512 devices in a mesh: dp: 16 (over z, y_lo), tile: 32 (over x, y_hi, core).
Axes of the slice: x: 4, y: 8 (y_hi: 4, y_lo: 2; y = y_hi * 2 + y_lo), z: 8, core: 2. Of those that a mesh axis runs over, the one named last changes fastest.
Arguments:
- acts: bfloat16 [2048, 4096], P('dp', 'tile'), may hold values from -64 to 64
- grads: bfloat16 [2048, 14336], P('dp', 'tile'), may hold values from -64 to 64
- basis_in: bfloat16 [4096, 4096], P('tile', 'dp'), may hold values from -0.09375 to 0.09375
- basis_out: bfloat16 [14336, 14336], P('dp', 'tile'), may hold values from -0.046875 to 0.046875
Outputs:
- act_cov: float32 [4096, 4096], P('tile', 'dp')
- grad_cov: float32 [14336, 14336], P('tile', 'dp')
- corrections: float32 [14336, 4096], P('tile', 'dp')
The draws below stay inside these ranges and needn't reach their ends.
All inputs are finite; a program needn't handle non-finite values.
Results may differ from the reference program's by a relative error of at most 0.0006.
Values may be sent and summed in bfloat16 or wider, within the bound.
A program may use at most 64 MiB of HBM per device.

```python
import jax
import jax.numpy as jnp

DIN = 4096
DOUT = 14336
TOKENS = 2048


def token_factor(rows):
    position = jnp.arange(rows, dtype=jnp.float32)
    return 0.5 + position / max(rows - 1, 1)


def scaled_table(key, rows, cols):
    key_base, key_cols, key_rows = jax.random.split(key, 3)
    col_scale = jnp.exp(jax.random.uniform(key_cols, (1, cols), jnp.float32, -1.15, 1.15))
    row_scale = jnp.exp(jax.random.uniform(key_rows, (rows, 1), jnp.float32, -0.7, 0.7))
    row_scale = row_scale * token_factor(rows)[:, None]
    normal_part = jnp.clip(jax.random.normal(key_base, (rows, cols), jnp.float32), -5.0, 5.0)
    return (normal_part, row_scale * col_scale)


def draw_acts(key, part):
    key = jax.random.fold_in(key, 11)
    normal_part, scales = scaled_table(key, TOKENS, DIN)
    base = normal_part
    return (base * scales).astype(jnp.bfloat16)


def draw_grads(key, part):
    key = jax.random.fold_in(key, 23)
    normal_part, scales = scaled_table(key, TOKENS, DOUT)
    base = normal_part
    return (base * scales).astype(jnp.bfloat16)


def shard_levels(key, extent, cuts, smallest, top_value):
    def one(dim, shards_of):
        heights = jax.random.uniform(jax.random.fold_in(jax.random.fold_in(key, 6), dim), (shards_of,), jnp.float32, smallest / len(cuts), top_value / len(cuts))
        return jnp.repeat(jnp.exp(heights), extent[dim] // shards_of).reshape((-1,) + (1,) * (len(extent) - dim - 1))

    gain = one(*cuts[0])
    for cut in cuts[1:]:
        gain = gain * one(*cut)
    return gain


def noise(own_key, shape, spread, bound, shards=(), kind=jnp.bfloat16):
    values = jax.random.normal(own_key, shape, jnp.float32) * spread
    if len(shards) > 0:
        values = shard_levels(own_key, shape, shards, -0.22, 0.18) * values
    return jnp.clip(values, min=-bound, max=bound).astype(kind)


def setup_inputs(seed: int = 0) -> dict:
    keys = jax.random.split(jax.random.key(seed), 5)
    return {
        "acts": draw_acts(jax.random.fold_in(keys[4], 71), 0),
        "grads": draw_grads(jax.random.fold_in(keys[4], 71), 0),
        "basis_in": noise(keys[2], (DIN, DIN), DIN ** -0.5, 0.09375, ((0, 32), (1, 16))),
        "basis_out": noise(keys[3], (DOUT, DOUT), DOUT ** -0.5, 0.046875, ((0, 16), (1, 32))),
    }


def reference(acts, grads, basis_in, basis_out):
    scale = 1.0 / TOKENS
    act_cov = jnp.dot(acts.T, acts, preferred_element_type=jnp.float32) * scale
    grad_cov = jnp.dot(grads.T, grads, preferred_element_type=jnp.float32) * scale
    proj_out = jnp.dot(grads, basis_out, preferred_element_type=jnp.float32)
    proj_in = jnp.dot(acts, basis_in, preferred_element_type=jnp.float32)
    sq_out = (proj_out * proj_out).astype(jnp.bfloat16)
    sq_in = (proj_in * proj_in).astype(jnp.bfloat16)
    corrections = jnp.dot(sq_out.T, sq_in, preferred_element_type=jnp.float32) * scale
    return act_cov, grad_cov, corrections
```

```python
import functools

import jax
import jax.numpy as jnp
from jax import lax
from jax.experimental import pallas as pl
from jax.experimental.pallas import tpu as pltpu
from jax.sharding import PartitionSpec as P

MESH = pl.DeviceIdType.MESH
F32 = jnp.float32
BF16 = jnp.bfloat16

G = 448
A = 128
R = G + A
Q = R // 4
B = 128
NB = 16
GH = G // 2
RH = R // 2

CHAIN = 1
K1, K2, K3 = 1, 2, 3
T_AT = (2, 5, 8, 11)
STEPS = 8 + 3 * CHAIN + K3


def mod(a, n):
    return (a + n) % n


def nt(a, b):
    return lax.dot_general(a, b, (((1,), (1,)), ((), ())), preferred_element_type=F32)


def nn(a, b):
    return lax.dot_general(a, b, (((1,), (0,)), ((), ())), preferred_element_type=F32)


def arrived(ref, sem):
    pltpu.make_async_copy(ref, ref, sem).wait()


def offset(g):
    half = (g + 1) // 2
    return 4 + half * (1 - 2 * (g % 2))


def kernel(
    acts, grads, basis_in, basis_out, act_cov, grad_cov, corr,
    xk, a1, xd, bt, bit, pf, pb, rb, rsu, rsd, sq, pio, pis, pir, px, py, si,
    a1_s, a1_r, own_sem, d2_s, y_r, ch_s, x_s, x_r, x2_s, x2_r, c_s, c_r,
    tp_s, tp_r, t_s, t_r, pr_s, pr_r, rs_s, rs_r, gp_s, gp_r, g_s, g_r,
    in_s, in_r,
):
    dp, tile = lax.axis_index("dp"), lax.axis_index("tile")
    z, yl = dp // 2, dp % 2
    k, c = tile // 2, tile % 2
    x, yh = k // 4, k % 4
    up, down = mod(z + 1, 8), mod(z + 7, 8)

    def at(z=z, yl=yl, x=x, yh=yh, c=c):
        return (2 * z + yl, (4 * x + yh) * 2 + c)

    def remote(src, dst, ss, rs, dev):
        return pltpu.make_async_remote_copy(
            src_ref=src, dst_ref=dst, send_sem=ss, recv_sem=rs, device_id=dev, device_id_type=MESH
        )

    sent = []

    def send(src, dst, ss, rs, dev):
        remote(src, dst, ss, rs, dev).start()
        sent.append((src, ss))

    xk[dp, 0:G] = grads[...].T
    xk[dp, G:R] = acts[...].T

    barrier = pltpu.get_barrier_semaphore()

    def greet(j, carry):
        pl.semaphore_signal(barrier, inc=1, device_id=(mod(dp + j, 16), tile), device_id_type=MESH)
        return carry

    lax.fori_loop(1, 16, greet, 0)
    for j in range(1, 4):
        pl.semaphore_signal(barrier, inc=1, device_id=at(x=mod(x + j, 4)), device_id_type=MESH)
        pl.semaphore_signal(barrier, inc=1, device_id=at(yh=mod(yh + j, 4)), device_id_type=MESH)
    pl.semaphore_signal(barrier, inc=1, device_id=at(c=1 - c), device_id_type=MESH)
    pl.semaphore_wait(barrier, 22)

    def quarter(ref, q):
        return ref.at[pl.ds(pl.multiple_of(q * Q, 16), Q)]

    for j in range(1, 4):
        q = mod(x + j, 4)
        send(quarter(xk.at[dp], q), a1.at[x], a1_s.at[j - 1], a1_r.at[x], at(x=q))
    keep = pltpu.make_async_copy(quarter(xk.at[dp], x), a1.at[x], own_sem)
    keep.start()
    keep.wait()

    def plane_of(col):
        return 2 * col + yh // 2, yh % 2

    def to_plane(j, act):
        col = mod(x + j, 4)
        zt, yt = plane_of(col)
        here = jnp.logical_and(zt == z, yt == yl)
        src, dst = a1.at[col], quarter(xd.at[c, dp], x)

        @pl.when(here)
        def _():
            if act:
                pltpu.make_async_copy(src, dst, y_r.at[dp]).start()

        @pl.when(jnp.logical_not(here))
        def _():
            copy = remote(src, dst, d2_s.at[j], y_r.at[dp], at(z=zt, yl=yt))
            if act:
                copy.start()
            else:
                copy.wait_send()

    for j in range(4):
        if j:
            col = mod(x + j, 4)
            arrived(a1.at[col], a1_r.at[col])
        to_plane(j, True)

    def ring_send(buf, rows, s, r, h, y, act=True):
        eu = 2 * mod(z - h, 8) + y
        ed = 2 * mod(z + h, 8) + y
        lo = pl.ds(0, rows if h < 3 else rows // 2)
        hi = pl.ds(0, rows) if h < 3 else pl.ds(rows // 2, rows // 2)
        for n, ref, dev in ((0, buf.at[eu, lo], at(z=up)), (1, buf.at[ed, hi], at(z=down))):
            copy = remote(ref, ref, s.at[n, h, y], r.at[n, h, y], dev)
            copy.start() if act else copy.wait_send()

    def ring_wait(buf, rows, r, h, y):
        eu = 2 * mod(z - 1 - h, 8) + y
        ed = 2 * mod(z + 1 + h, 8) + y
        lo = pl.ds(0, rows if h < 3 else rows // 2)
        hi = pl.ds(0, rows) if h < 3 else pl.ds(rows // 2, rows // 2)
        arrived(buf.at[eu, lo], r.at[0, h, y])
        arrived(buf.at[ed, hi], r.at[1, h, y])

    def ring_hop(buf, rows, s, r, h):
        for y in (yl, 1 - yl):
            ring_wait(buf, rows, r, h - 1, y)
            if h < 4:
                ring_send(buf, rows, s, r, h, y)

    send(xk.at[dp], xk.at[dp], tp_s, tp_r, at(yl=1 - yl))
    ring_send(xk, R, t_s, t_r, 0, yl)

    bt[...] = basis_out[...].T
    bit[...] = basis_in[...].T
    partner = 2 * z + 1 - yl
    arrived(xk.at[partner], tp_r)
    ring_send(xk, R, t_s, t_r, 0, 1 - yl)

    root = 2 * (z % 2) + yl
    role = mod(yh - root, 4)
    hops = (role, mod(4 - role, 4))
    last = jnp.maximum(hops[0], hops[1])

    def stage(f, i, late):
        g = i - hops[f] * CHAIN - late
        e = 2 * mod(z + offset(g) + 8, 8) + f
        return jnp.logical_and(g >= 0, g < 8), e

    right, left = mod(x + 1, 4), mod(x + 3, 4)
    west, east = at(x=left), at(x=right)

    def spread(f, e, act):
        mine = quarter(xd.at[c, e], x)
        if act:
            arrived(mine, y_r.at[e])

        @pl.when(hops[f] < 3)
        def _():
            step = 1 if f == 0 else 3
            copy = remote(mine, mine, ch_s.at[e], y_r.at[e], at(yh=mod(yh + step, 4)))
            copy.start() if act else copy.wait_send()

        for n, dev in enumerate((east, west)):
            copy = remote(mine, mine, x_s.at[n, e], x_r.at[n, e], dev)
            copy.start() if act else copy.wait_send()

    def across(f, e, act):
        from_left, from_right = quarter(xd.at[c, e], left), quarter(xd.at[c, e], right)
        if act:
            arrived(from_left, x_r.at[0, e])
            arrived(from_right, x_r.at[1, e])
        ref, dev = (from_left, east) if f == 0 else (from_right, west)
        copy = remote(ref, ref, x2_s.at[e], x2_r.at[e], dev)
        copy.start() if act else copy.wait_send()

    def share(f, e, act):
        if act:
            arrived(quarter(xd.at[c, e], mod(x + 2, 4)), x2_r.at[e])
        copy = remote(xd.at[c, e], xd.at[c, e], c_s.at[e], c_r.at[e], at(c=1 - c))
        copy.start() if act else copy.wait_send()

    def project(g):
        zz = mod(z + offset(g) + 8, 8)
        cols = []
        for f in range(2):
            arrived(xd.at[1 - c, 2 * zz + f], c_r.at[2 * zz + f])
        for f in range(2):
            cols.append(jnp.concatenate([xd[0, 2 * zz + f, 0:G], xd[1, 2 * zz + f, 0:G]], axis=0))
        out = nn(bt[...], jnp.concatenate(cols, axis=1))
        first, second = out[:, 0:B], out[:, B : 2 * B]
        even = yl == 0
        pf[zz] = jnp.where(even, first, second)
        pb[zz] = jnp.where(even, second, first).astype(BF16)
        remote(pb.at[zz], rb.at[zz], pr_s.at[zz], pr_r.at[zz], at(yl=1 - yl)).start()

    def step(i, carry):
        for f in range(2):
            for late, work in ((0, spread), (K1, across), (K2, share)):
                valid, e = stage(f, i, late)

                @pl.when(valid)
                def _():
                    work(f, e, True)

        for n, when in enumerate(T_AT):

            @pl.when(i == when)
            def _():
                ring_hop(xk, R, t_s, t_r, n + 1)

        g = i - last * CHAIN - K3

        @pl.when(jnp.logical_and(g >= 0, g < 8))
        def _():
            project(g)

        return carry

    lax.fori_loop(0, STEPS, step, 0)

    def total(zz):
        arrived(rb.at[zz], pr_r.at[zz])
        return pf[zz] + rb[zz].astype(F32)

    far = mod(z + 4, 8)
    pf[far] = total(far)
    send(pf.at[far, 0:GH], rsu.at[0, 0:GH], rs_s.at[0, 0], rs_r.at[0, 0], at(z=up))
    send(pf.at[far, GH:G], rsd.at[0, GH:G], rs_s.at[1, 0], rs_r.at[1, 0], at(z=down))

    def reduce_step(s):
        for n, (buf, zz, dev) in enumerate(
            ((rsu, mod(z + 4 - s, 8), at(z=up)), (rsd, mod(z + 4 + s, 8), at(z=down)))
        ):
            pf[zz] = total(zz)
            rows = slice(0, G) if s > 1 else (slice(0, GH), slice(GH, G))[n]
            arrived(buf.at[s - 1, rows], rs_r.at[n, s - 1])
            pf[zz, rows] = pf[zz, rows] + buf[s - 1, rows]
            send(pf.at[zz], buf.at[s], rs_s.at[n, s], rs_r.at[n, s], dev)

    def project_in():
        mine = bit[pl.ds(pl.multiple_of(c * A, A), A)]
        other = bit[pl.ds(pl.multiple_of((1 - c) * A, A), A)]
        for e in range(0, NB, 4):
            cols = jnp.concatenate([xk[e + n, G:R] for n in range(4)], axis=1)
            for weights, ref in ((mine, pio), (other, pis)):
                out = nn(weights, cols)
                for n in range(4):
                    ref[e + n] = out[:, n * B : (n + 1) * B]
        send(pis, pir, in_s.at[0], in_r.at[0], at(c=1 - c))

    def in_over_x():
        arrived(pir, in_r.at[0])
        pio[...] = pio[...] + pir[...]
        for j in range(1, 4):
            q = mod(x + j, 4)
            send(pio.at[pl.ds(4 * q, 4)], px.at[x], in_s.at[j], in_r.at[1 + x], at(x=q))

    def in_over_y():
        mine = pl.ds(4 * x, 4)
        acc = pio[mine]
        for j in range(1, 4):
            q = mod(x + j, 4)
            arrived(px.at[q], in_r.at[1 + q])
            acc = acc + px[q]
        pio[mine] = acc
        for j in range(1, 4):
            w = mod(yh + j, 4)
            send(pio.at[4 * x + w], py.at[yh], in_s.at[3 + j], in_r.at[5 + yh], at(yh=w))

    def in_square():
        acc = pio[k]
        for j in range(1, 4):
            w = mod(yh + j, 4)
            arrived(py.at[w], in_r.at[5 + w])
            acc = acc + py[w]
        si[c, k] = (acc * acc).astype(BF16)
        for j in range(1, 4):
            w = mod(yh + j, 4)
            send(si.at[c, k], si.at[c, k], in_s.at[6 + j], in_r.at[9 + yh], at(yh=w))

    def in_gather_x():
        for j in range(1, 4):
            w = mod(yh + j, 4)
            arrived(si.at[c, 4 * x + w], in_r.at[9 + w])
        mine = si.at[c, pl.ds(4 * x, 4)]
        for j in range(1, 4):
            q = mod(x + j, 4)
            send(mine, mine, in_s.at[9 + j], in_r.at[13 + x], at(x=q))

    def in_share():
        for j in range(1, 4):
            q = mod(x + j, 4)
            arrived(si.at[c, pl.ds(4 * q, 4)], in_r.at[13 + q])
        send(si.at[c], si.at[c], in_s.at[13], in_r.at[17], at(c=1 - c))

    scale = 1.0 / (NB * B)

    def covariances(first):
        for e in (first, first + 4):
            blocks = range(e, e + 4)
            rows = jnp.concatenate([xk[n, 0:G] for n in blocks], axis=1)
            cols = jnp.concatenate(
                [jnp.concatenate([xd[0, n, 0:G], xd[1, n, 0:G]], axis=0) for n in blocks], axis=1
            )
            part = nt(rows, cols) * scale
            grad_cov[...] = part if e == 0 else grad_cov[...] + part
            rows = jnp.concatenate([xk[n, G:R] for n in blocks], axis=1)
            cols = jnp.concatenate(
                [jnp.concatenate([xd[0, n, G:R], xd[1, n, G:R]], axis=0) for n in blocks], axis=1
            )
            part = nt(rows, cols) * scale
            act_cov[...] = part if e == 0 else act_cov[...] + part

    project_in()
    reduce_step(1)
    in_over_x()
    reduce_step(2)
    covariances(0)
    reduce_step(3)
    in_over_y()

    arrived(rsu.at[3], rs_r.at[0, 3])
    arrived(rsd.at[3], rs_r.at[1, 3])
    mine = total(z) + rsu[3] + rsd[3]
    sq[dp] = (mine * mine).astype(BF16)

    send(sq.at[dp], sq.at[dp], gp_s, gp_r, at(yl=1 - yl))
    ring_send(sq, G, g_s, g_r, 0, yl)
    arrived(sq.at[partner], gp_r)
    ring_send(sq, G, g_s, g_r, 0, 1 - yl)
    in_square()
    ring_hop(sq, G, g_s, g_r, 1)
    in_gather_x()
    covariances(8)
    ring_hop(sq, G, g_s, g_r, 2)
    in_share()
    ring_hop(sq, G, g_s, g_r, 3)
    arrived(si.at[1 - c], in_r.at[17])
    ring_hop(sq, G, g_s, g_r, 4)

    for e in range(0, NB, 4):
        blocks = range(e, e + 4)
        rows = jnp.concatenate([sq[n] for n in blocks], axis=1)
        cols = jnp.concatenate(
            [jnp.concatenate([si[0, n], si[1, n]], axis=0) for n in blocks], axis=1
        )
        part = nt(rows, cols) * scale
        corr[...] = part if e == 0 else corr[...] + part

    for src, sem in sent:
        arrived(src, sem)
    for j in range(4):
        to_plane(j, False)
    for h in range(4):
        for y in range(2):
            ring_send(xk, R, t_s, t_r, h, y, False)
            ring_send(sq, G, g_s, g_r, h, y, False)

    def finish(g, carry):
        for f in range(2):
            e = 2 * g + f
            spread(f, e, False)
            across(f, e, False)
            share(f, e, False)
        arrived(pb.at[g], pr_s.at[g])
        return carry

    lax.fori_loop(0, 8, finish, 0)


def body(acts, grads, basis_in, basis_out):
    vmem = pl.BlockSpec(memory_space=pltpu.VMEM)
    dma = pltpu.SemaphoreType.DMA
    return pl.pallas_call(
        kernel,
        out_shape=(
            jax.ShapeDtypeStruct((A, 2 * A), F32),
            jax.ShapeDtypeStruct((G, 2 * G), F32),
            jax.ShapeDtypeStruct((G, 2 * A), F32),
        ),
        in_specs=[vmem] * 4,
        out_specs=(vmem,) * 3,
        scratch_shapes=[
            pltpu.VMEM((NB, R, B), BF16),
            pltpu.VMEM((4, Q, B), BF16),
            pltpu.VMEM((2, NB, R, B), BF16),
            pltpu.VMEM((G, 2 * G), BF16),
            pltpu.VMEM((2 * A, A), BF16),
            pltpu.VMEM((8, G, B), F32),
            pltpu.VMEM((8, G, B), BF16),
            pltpu.VMEM((8, G, B), BF16),
            pltpu.VMEM((4, G, B), F32),
            pltpu.VMEM((4, G, B), F32),
            pltpu.VMEM((NB, G, B), BF16),
            pltpu.VMEM((NB, A, B), F32),
            pltpu.VMEM((NB, A, B), F32),
            pltpu.VMEM((NB, A, B), F32),
            pltpu.VMEM((4, 4, A, B), F32),
            pltpu.VMEM((4, A, B), F32),
            pltpu.VMEM((2, NB, A, B), BF16),
            dma((3,)), dma((4,)), dma, dma((4,)), dma((NB,)), dma((NB,)),
            dma((2, NB)), dma((2, NB)), dma((NB,)), dma((NB,)), dma((NB,)), dma((NB,)),
            dma, dma, dma((2, 4, 2)), dma((2, 4, 2)), dma((8,)), dma((8,)),
            dma((2, 4)), dma((2, 4)), dma, dma, dma((2, 4, 2)), dma((2, 4, 2)),
            dma((14,)), dma((18,)),
        ],
        compiler_params=pltpu.CompilerParams(
            collective_id=0, has_side_effects=True, vmem_limit_bytes=52 << 20
        ),
        name="ekfac",
    )(acts, grads, basis_in, basis_out)


def solution(mesh):
    in_specs = (P("dp", "tile"), P("dp", "tile"), P("tile", "dp"), P("dp", "tile"))
    out_specs = (P("tile", "dp"), P("tile", "dp"), P("tile", "dp"))
    return jax.shard_map(body, mesh=mesh, in_specs=in_specs, out_specs=out_specs, check_vma=False)
```

```python
import functools

import jax
import jax.numpy as jnp
from jax import lax
from jax.experimental import pallas as pl
from jax.experimental.pallas import tpu as pltpu
from jax.sharding import PartitionSpec as P

MESH = pl.DeviceIdType.MESH
F32 = jnp.float32
BF16 = jnp.bfloat16

G = 448
A = 128
R = G + A
Q = R // 4
B = 128
NB = 16
GH = G // 2
RH = R // 2

CHAIN = 2
K1, K2, K3 = 2, 4, 5
PROJECT = 3 * CHAIN + K3
STEPS = 8 + PROJECT
GATHER_AT = (3, 6, 9, 12)
REDUCE_AT = tuple(PROJECT + 1 + 2 * s for s in range(4))
INPUT_AT = (13, 15)


def mod(a, n):
    return (a + n) % n


def nt(a, b):
    return lax.dot_general(a, b, (((1,), (1,)), ((), ())), preferred_element_type=F32)


def nn(a, b):
    return lax.dot_general(a, b, (((1,), (0,)), ((), ())), preferred_element_type=F32)


def arrived(ref, sem):
    pltpu.make_async_copy(ref, ref, sem).wait()


def offset(g):
    half = (g + 1) // 2
    return 4 + half * (1 - 2 * (g % 2))


def kernel(
    acts, grads_t, basis_in, basis_out_t, act_cov, grad_out, corr,
    xk, a1, xd, bt, bit, grad_cov, pf, pb, rb, rsu, rsd, sq, pio, pis, pir, px, py, si,
    a1_s, a1_r, own_sem, d2_s, y_r, ch_s, x_s, x_r, x2_s, x2_r, c_s, c_r,
    tp_s, tp_r, t_s, t_r, pr_s, pr_r, rs_s, rs_r, gp_s, gp_r, g_s, g_r, gb_s, gb_r,
    in_s, in_r,
):
    dp, tile = lax.axis_index("dp"), lax.axis_index("tile")
    z, yl = dp // 2, dp % 2
    k, c = tile // 2, tile % 2
    x, yh = k // 4, k % 4
    up, down = mod(z + 1, 8), mod(z + 7, 8)
    partner = 2 * z + 1 - yl

    def at(z=z, yl=yl, x=x, yh=yh, c=c):
        return (2 * z + yl, (4 * x + yh) * 2 + c)

    def remote(src, dst, ss, rs, dev):
        return pltpu.make_async_remote_copy(
            src_ref=src, dst_ref=dst, send_sem=ss, recv_sem=rs, device_id=dev, device_id_type=MESH
        )

    def send(act, src, dst, ss, rs, dev):
        copy = remote(src, dst, ss, rs, dev)
        copy.start() if act else copy.wait_send()

    barrier = pltpu.get_barrier_semaphore()

    def greet(j, carry):
        pl.semaphore_signal(barrier, inc=1, device_id=(mod(dp + j, 16), tile), device_id_type=MESH)
        return carry

    lax.fori_loop(1, 16, greet, 0)
    for j in range(1, 4):
        pl.semaphore_signal(barrier, inc=1, device_id=at(x=mod(x + j, 4)), device_id_type=MESH)
        pl.semaphore_signal(barrier, inc=1, device_id=at(yh=mod(yh + j, 4)), device_id_type=MESH)
    pl.semaphore_signal(barrier, inc=1, device_id=at(c=1 - c), device_id_type=MESH)

    own_grads = pltpu.make_async_copy(grads_t, xk.at[dp, pl.ds(0, G)], own_sem.at[0])
    own_grads.start()
    weights = pltpu.make_async_copy(basis_out_t, bt, own_sem.at[1])
    weights.start()
    xk[dp, G:R] = acts[...].T
    own_grads.wait()
    pl.semaphore_wait(barrier, 22)

    def quarter(ref, q):
        return ref.at[pl.ds(pl.multiple_of(q * Q, 16), Q)]

    def over_x(act):
        for j in range(1, 4):
            q = mod(x + j, 4)
            send(act, quarter(xk.at[dp], q), a1.at[x], a1_s.at[j - 1], a1_r.at[x], at(x=q))

    over_x(True)
    keep = pltpu.make_async_copy(quarter(xk.at[dp], x), a1.at[x], own_sem.at[2])
    keep.start()
    keep.wait()

    def plane_of(col):
        return 2 * col + yh // 2, yh % 2

    def to_plane(j, act):
        col = mod(x + j, 4)
        zt, yt = plane_of(col)
        here = jnp.logical_and(zt == z, yt == yl)
        src, dst = a1.at[col], quarter(xd.at[c, dp], x)

        @pl.when(here)
        def _():
            if act:
                pltpu.make_async_copy(src, dst, y_r.at[dp]).start()

        @pl.when(jnp.logical_not(here))
        def _():
            send(act, src, dst, d2_s.at[j], y_r.at[dp], at(z=zt, yl=yt))

    for j in range(4):
        if j:
            col = mod(x + j, 4)
            arrived(a1.at[col], a1_r.at[col])
        to_plane(j, True)

    def ring_refs(buf, h, y, low, rows, far):
        zu, zd = mod(z - h, 8), mod(z + h, 8)
        if h < 3:
            a = b = pl.ds(low, rows)
        else:
            a, b = pl.ds(low, far), pl.ds(low + far, rows - far)
        return buf.at[2 * zu + y, a], buf.at[2 * zd + y, b]

    def ring_send(act, buf, s, r, h, y, p, low, rows):
        for n, ref, dev in zip((0, 1), ring_refs(buf, h, y, low, rows, rows // 2), (up, down)):
            send(act, ref, ref, s.at[n, h, p], r.at[n, h, p], at(z=dev))

    def ring_wait(buf, r, h, y, p, low, rows):
        zu, zd = mod(z - 1 - h, 8), mod(z + 1 + h, 8)
        half = rows // 2
        a = pl.ds(low, rows if h < 3 else half)
        b = pl.ds(low, rows) if h < 3 else pl.ds(low + half, half)
        arrived(buf.at[2 * zu + y, a], r.at[0, h, p])
        arrived(buf.at[2 * zd + y, b], r.at[1, h, p])

    def columns_pair(act):
        send(act, xk.at[dp], xk.at[dp], tp_s, tp_r, at(yl=1 - yl))

    def columns_send(act, h, p):
        ring_send(act, xk, t_s, t_r, h, yl if p == 0 else 1 - yl, p, 0, R)

    def columns_hop(h):
        for p in range(2):
            ring_wait(xk, t_r, h - 1, yl if p == 0 else 1 - yl, p, 0, R)
            if h < 4:
                columns_send(True, h, p)

    columns_pair(True)
    columns_send(True, 0, 0)
    bit[...] = basis_in[...].T
    weights.wait()
    arrived(xk.at[partner], tp_r)
    columns_send(True, 0, 1)

    root = 2 * (z % 2) + yl
    role = mod(yh - root, 4)
    hops = (role, mod(4 - role, 4))

    def stage(f, i, late):
        g = i - hops[f] * CHAIN - late
        e = 2 * mod(z + offset(g) + 8, 8) + f
        return jnp.logical_and(g >= 0, g < 8), e

    right, left = mod(x + 1, 4), mod(x + 3, 4)
    west, east = at(x=left), at(x=right)

    def spread(f, e, act):
        mine = quarter(xd.at[c, e], x)
        if act:
            arrived(mine, y_r.at[e])

        @pl.when(hops[f] < 3)
        def _():
            step = 1 if f == 0 else 3
            copy = remote(mine, mine, ch_s.at[e], y_r.at[e], at(yh=mod(yh + step, 4)))
            copy.start() if act else copy.wait_send()

        for n, dev in enumerate((east, west)):
            copy = remote(mine, mine, x_s.at[n, e], x_r.at[n, e], dev)
            copy.start() if act else copy.wait_send()

    def across(f, e, act):
        from_left, from_right = quarter(xd.at[c, e], left), quarter(xd.at[c, e], right)
        if act:
            arrived(from_left, x_r.at[0, e])
            arrived(from_right, x_r.at[1, e])
        ref, dev = (from_left, east) if f == 0 else (from_right, west)
        copy = remote(ref, ref, x2_s.at[e], x2_r.at[e], dev)
        copy.start() if act else copy.wait_send()

    def share(f, e, act):
        if act:
            arrived(quarter(xd.at[c, e], mod(x + 2, 4)), x2_r.at[e])
        copy = remote(xd.at[c, e], xd.at[c, e], c_s.at[e], c_r.at[e], at(c=1 - c))
        copy.start() if act else copy.wait_send()

    def pair(zz, act):
        send(act, pb.at[zz], rb.at[zz], pr_s.at[zz], pr_r.at[zz], at(yl=1 - yl))

    def project(g):
        zz = mod(z + offset(g) + 8, 8)
        cols = []
        for f in range(2):
            arrived(xd.at[1 - c, 2 * zz + f], c_r.at[2 * zz + f])
        for f in range(2):
            cols.append(jnp.concatenate([xd[0, 2 * zz + f, 0:G], xd[1, 2 * zz + f, 0:G]], axis=0))
        out = nn(bt[...], jnp.concatenate(cols, axis=1))
        first, second = out[:, 0:B], out[:, B : 2 * B]
        even = yl == 0
        pf[zz] = jnp.where(even, first, second)
        pb[zz] = jnp.where(even, second, first).astype(BF16)
        pair(zz, True)

    def total(zz):
        arrived(rb.at[zz], pr_r.at[zz])
        return pf[zz] + rb[zz].astype(F32)

    def reduce_send(act, s):
        if s == 0:
            far = mod(z + 4, 8)
            if act:
                pf[far] = total(far)
            send(act, pf.at[far, 0:GH], rsu.at[0, 0:GH], rs_s.at[0, 0], rs_r.at[0, 0], at(z=up))
            send(act, pf.at[far, GH:G], rsd.at[0, GH:G], rs_s.at[1, 0], rs_r.at[1, 0], at(z=down))
            return
        for n, (buf, zz, dev) in enumerate(
            ((rsu, mod(z + 4 - s, 8), at(z=up)), (rsd, mod(z + 4 + s, 8), at(z=down)))
        ):
            if act:
                rows = slice(0, G) if s > 1 else (slice(0, GH), slice(GH, G))[n]
                pf[zz] = total(zz)
                arrived(buf.at[s - 1, rows], rs_r.at[n, s - 1])
                pf[zz, rows] = pf[zz, rows] + buf[s - 1, rows]
            send(act, pf.at[zz], buf.at[s], rs_s.at[n, s], rs_r.at[n, s], dev)

    def project_in(act):
        if act:
            mine = bit[pl.ds(pl.multiple_of(c * A, A), A)]
            other = bit[pl.ds(pl.multiple_of((1 - c) * A, A), A)]
            for e in range(0, NB, 4):
                cols = jnp.concatenate([xk[e + n, G:R] for n in range(4)], axis=1)
                for weights, ref in ((mine, pio), (other, pis)):
                    out = nn(weights, cols)
                    for n in range(4):
                        ref[e + n] = out[:, n * B : (n + 1) * B]
        send(act, pis, pir, in_s.at[0], in_r.at[0], at(c=1 - c))

    def in_over_x(act):
        if act:
            arrived(pir, in_r.at[0])
            pio[...] = pio[...] + pir[...]
        for j in range(1, 4):
            q = mod(x + j, 4)
            send(act, pio.at[pl.ds(4 * q, 4)], px.at[x], in_s.at[j], in_r.at[1 + x], at(x=q))

    def in_over_y(act):
        mine = pl.ds(4 * x, 4)
        if act:
            acc = pio[mine]
            for j in range(1, 4):
                q = mod(x + j, 4)
                arrived(px.at[q], in_r.at[1 + q])
                acc = acc + px[q]
            pio[mine] = acc
        for j in range(1, 4):
            w = mod(yh + j, 4)
            send(act, pio.at[4 * x + w], py.at[yh], in_s.at[3 + j], in_r.at[5 + yh], at(yh=w))

    def in_square(act):
        if act:
            acc = pio[k]
            for j in range(1, 4):
                w = mod(yh + j, 4)
                arrived(py.at[w], in_r.at[5 + w])
                acc = acc + py[w]
            si[c, k] = (acc * acc).astype(BF16)
        for j in range(1, 4):
            w = mod(yh + j, 4)
            send(act, si.at[c, k], si.at[c, k], in_s.at[6 + j], in_r.at[9 + yh], at(yh=w))

    def in_gather_x(act):
        if act:
            for j in range(1, 4):
                w = mod(yh + j, 4)
                arrived(si.at[c, 4 * x + w], in_r.at[9 + w])
        mine = si.at[c, pl.ds(4 * x, 4)]
        for j in range(1, 4):
            q = mod(x + j, 4)
            send(act, mine, mine, in_s.at[9 + j], in_r.at[13 + x], at(x=q))

    def in_share(act):
        if act:
            for j in range(1, 4):
                q = mod(x + j, 4)
                arrived(si.at[c, pl.ds(4 * q, 4)], in_r.at[13 + q])
        send(act, si.at[c], si.at[c], in_s.at[13], in_r.at[17], at(c=1 - c))

    def squares_send(act, h, p):
        if p == 0:
            ring_send(act, sq, g_s, g_r, h, yl, 0, 0, G)
        else:
            ring_send(act, sq, g_s, g_r, h, 1 - yl, 1, 0, GH)

    def lower(act, zz):
        ref = sq.at[2 * zz + yl, GH:G]
        send(act, ref, ref, gb_s.at[zz], gb_r.at[zz], at(yl=1 - yl))

    def upper(act):
        ref = sq.at[dp, 0:GH]
        send(act, ref, ref, gp_s, gp_r, at(yl=1 - yl))

    def squares_hop(h):
        ring_wait(sq, g_r, h - 1, yl, 0, 0, G)
        if h < 4:
            squares_send(True, h, 0)
        for zz in (mod(z - h, 8), mod(z + h, 8))[: 2 if h < 4 else 1]:
            lower(True, zz)
        ring_wait(sq, g_r, h - 1, 1 - yl, 1, 0, GH)
        if h < 4:
            squares_send(True, h, 1)

    scale = 1.0 / (NB * B)

    def covariances(first):
        for e in (first, first + 4):
            blocks = range(e, e + 4)
            rows = jnp.concatenate([xk[n, 0:G] for n in blocks], axis=1)
            cols = jnp.concatenate(
                [jnp.concatenate([xd[0, n, 0:G], xd[1, n, 0:G]], axis=0) for n in blocks], axis=1
            )
            part = nt(rows, cols) * scale
            grad_cov[...] = part if e == 0 else grad_cov[...] + part
            rows = jnp.concatenate([xk[n, G:R] for n in blocks], axis=1)
            cols = jnp.concatenate(
                [jnp.concatenate([xd[0, n, G:R], xd[1, n, G:R]], axis=0) for n in blocks], axis=1
            )
            part = nt(rows, cols) * scale
            act_cov[...] = part if e == 0 else act_cov[...] + part

    def store(act):
        copy = pltpu.make_async_copy(grad_cov, grad_out, own_sem.at[3])
        copy.start() if act else copy.wait()

    work = {}
    for n, when in enumerate(GATHER_AT):
        work.setdefault(when, []).append(functools.partial(columns_hop, n + 1))
    for n, when in enumerate(REDUCE_AT):
        work.setdefault(when, []).append(functools.partial(reduce_send, True, n))
    for when, fn in zip(INPUT_AT, (project_in, in_over_x)):
        work.setdefault(when, []).append(functools.partial(fn, True))

    def step(i, carry):
        for f in range(2):
            for late, fn in ((0, spread), (K1, across), (K2, share)):
                valid, e = stage(f, i, late)

                @pl.when(valid)
                def _():
                    fn(f, e, True)

        g = i - PROJECT

        @pl.when(jnp.logical_and(g >= 0, g < 8))
        def _():
            project(g)

        for when in sorted(work):
            if when < STEPS:

                @pl.when(i == when)
                def _():
                    for fn in work[when]:
                        fn()

        return carry

    lax.fori_loop(0, STEPS, step, 0)
    for when in sorted(work):
        if when >= STEPS:
            for fn in work[when]:
                fn()

    covariances(0)
    in_over_y(True)

    arrived(rsu.at[3], rs_r.at[0, 3])
    arrived(rsd.at[3], rs_r.at[1, 3])
    mine = total(z) + rsu[3] + rsd[3]
    sq[dp] = (mine * mine).astype(BF16)

    upper(True)
    squares_send(True, 0, 0)
    lower(True, z)
    arrived(sq.at[partner, 0:GH], gp_r)
    squares_send(True, 0, 1)
    in_square(True)
    squares_hop(1)
    in_gather_x(True)
    covariances(8)
    store(True)
    squares_hop(2)
    in_share(True)
    squares_hop(3)
    arrived(si.at[1 - c], in_r.at[17])
    squares_hop(4)
    for zz in range(8):
        arrived(sq.at[2 * zz + 1 - yl, GH:G], gb_r.at[zz])

    for e in range(0, NB, 4):
        blocks = range(e, e + 4)
        rows = jnp.concatenate([sq[n] for n in blocks], axis=1)
        cols = jnp.concatenate(
            [jnp.concatenate([si[0, n], si[1, n]], axis=0) for n in blocks], axis=1
        )
        part = nt(rows, cols) * scale
        corr[...] = part if e == 0 else corr[...] + part

    store(False)
    over_x(False)
    for j in range(4):
        to_plane(j, False)
    columns_pair(False)
    upper(False)
    for h in range(4):
        reduce_send(False, h)
        for p in range(2):
            columns_send(False, h, p)
            squares_send(False, h, p)
    for fn in (project_in, in_over_x, in_over_y, in_square, in_gather_x, in_share):
        fn(False)

    def finish(g, carry):
        for f in range(2):
            e = 2 * g + f
            spread(f, e, False)
            across(f, e, False)
            share(f, e, False)
        pair(g, False)
        lower(False, g)
        return carry

    lax.fori_loop(0, 8, finish, 0)


def body(acts, grads, basis_in, basis_out):
    vmem = pl.BlockSpec(memory_space=pltpu.VMEM)
    hbm = pl.BlockSpec(memory_space=pltpu.HBM)
    dma = pltpu.SemaphoreType.DMA
    shapes = (
        jax.ShapeDtypeStruct((A, 2 * A), F32),
        jax.ShapeDtypeStruct((G, 2 * G), F32),
        jax.ShapeDtypeStruct((G, 2 * A), F32),
    )
    return pl.pallas_call(
        kernel,
        out_shape=shapes,
        in_specs=[vmem, hbm, vmem, hbm],
        out_specs=(vmem, hbm, vmem),
        scratch_shapes=[
            pltpu.VMEM((NB, R, B), BF16),
            pltpu.VMEM((4, Q, B), BF16),
            pltpu.VMEM((2, NB, R, B), BF16),
            pltpu.VMEM((G, 2 * G), BF16),
            pltpu.VMEM((2 * A, A), BF16),
            pltpu.VMEM((G, 2 * G), F32),
            pltpu.VMEM((8, G, B), F32),
            pltpu.VMEM((8, G, B), BF16),
            pltpu.VMEM((8, G, B), BF16),
            pltpu.VMEM((4, G, B), F32),
            pltpu.VMEM((4, G, B), F32),
            pltpu.VMEM((NB, G, B), BF16),
            pltpu.VMEM((NB, A, B), F32),
            pltpu.VMEM((NB, A, B), F32),
            pltpu.VMEM((NB, A, B), F32),
            pltpu.VMEM((4, 4, A, B), F32),
            pltpu.VMEM((4, A, B), F32),
            pltpu.VMEM((2, NB, A, B), BF16),
            dma((3,)), dma((4,)), dma((4,)), dma((4,)), dma((NB,)), dma((NB,)),
            dma((2, NB)), dma((2, NB)), dma((NB,)), dma((NB,)), dma((NB,)), dma((NB,)),
            dma, dma, dma((2, 4, 2)), dma((2, 4, 2)), dma((8,)), dma((8,)),
            dma((2, 4)), dma((2, 4)), dma, dma, dma((2, 4, 2)), dma((2, 4, 2)), dma((8,)), dma((8,)),
            dma((14,)), dma((18,)),
        ],
        compiler_params=pltpu.CompilerParams(
            collective_id=0, has_side_effects=True, vmem_limit_bytes=62 << 20
        ),
        name="ekfac",
    )(acts, grads.T, basis_in, basis_out.T)


def solution(mesh):
    in_specs = (P("dp", "tile"), P("dp", "tile"), P("tile", "dp"), P("dp", "tile"))
    out_specs = (P("tile", "dp"), P("tile", "dp"), P("tile", "dp"))
    return jax.shard_map(body, mesh=mesh, in_specs=in_specs, out_specs=out_specs, check_vma=False)
```

```python
import functools

import jax
import jax.numpy as jnp
from jax import lax
from jax.experimental import pallas as pl
from jax.experimental.pallas import tpu as pltpu
from jax.sharding import PartitionSpec as P

MESH = pl.DeviceIdType.MESH
F32 = jnp.float32
BF16 = jnp.bfloat16

G = 448
A = 128
R = G + A
Q = R // 4
B = 128
NB = 16
GH = G // 2
GQ = G // 4

CHAIN = 2
K1, K2, K3 = 2, 4, 5
PROJECT = 3 * CHAIN + K3
STEPS = 8 + PROJECT
GATHER_AT = (3, 6, 9, 12)
REDUCE_AT = PROJECT + 1
INPUT_AT = (13, 15)


def mod(a, n):
    return (a + n) % n


def nt(a, b):
    return lax.dot_general(a, b, (((1,), (1,)), ((), ())), preferred_element_type=F32)


def nn(a, b):
    return lax.dot_general(a, b, (((1,), (0,)), ((), ())), preferred_element_type=F32)


def arrived(ref, sem):
    pltpu.make_async_copy(ref, ref, sem).wait()


def offset(g):
    half = (g + 1) // 2
    return 4 + half * (1 - 2 * (g % 2))


def kernel(
    acts, grads_t, basis_in, basis_out_t, act_cov, grad_out, corr,
    xk, a1, xd, bt, bit, grad_cov, pf, pb, rb, rsu, rsd, sq, pio, pis, pir, px, py, si,
    a1_s, a1_r, own_sem, d2_s, y_r, ch_s, x_s, x_r, x2_s, x2_r, c_s, c_r,
    tp_s, tp_r, t_s, t_r, pr_s, pr_r, rs_s, rs_r, gp_s, gp_r, g_s, g_r, gb_s, gb_r,
    in_s, in_r,
):
    dp, tile = lax.axis_index("dp"), lax.axis_index("tile")
    z, yl = dp // 2, dp % 2
    k, c = tile // 2, tile % 2
    x, yh = k // 4, k % 4
    up, down = mod(z + 1, 8), mod(z + 7, 8)
    partner = 2 * z + 1 - yl

    def at(z=z, yl=yl, x=x, yh=yh, c=c):
        return (2 * z + yl, (4 * x + yh) * 2 + c)

    def remote(src, dst, ss, rs, dev):
        return pltpu.make_async_remote_copy(
            src_ref=src, dst_ref=dst, send_sem=ss, recv_sem=rs, device_id=dev, device_id_type=MESH
        )

    def send(act, src, dst, ss, rs, dev):
        copy = remote(src, dst, ss, rs, dev)
        copy.start() if act else copy.wait_send()

    barrier = pltpu.get_barrier_semaphore()

    def greet(j, carry):
        pl.semaphore_signal(barrier, inc=1, device_id=(mod(dp + j, 16), tile), device_id_type=MESH)
        return carry

    lax.fori_loop(1, 16, greet, 0)
    for j in range(1, 4):
        pl.semaphore_signal(barrier, inc=1, device_id=at(x=mod(x + j, 4)), device_id_type=MESH)
        pl.semaphore_signal(barrier, inc=1, device_id=at(yh=mod(yh + j, 4)), device_id_type=MESH)
    pl.semaphore_signal(barrier, inc=1, device_id=at(c=1 - c), device_id_type=MESH)

    own_grads = pltpu.make_async_copy(grads_t, xk.at[dp, pl.ds(0, G)], own_sem.at[0])
    own_grads.start()
    weights = pltpu.make_async_copy(basis_out_t, bt, own_sem.at[1])
    weights.start()
    xk[dp, G:R] = acts[...].T
    own_grads.wait()
    pl.semaphore_wait(barrier, 22)

    def quarter(ref, q):
        return ref.at[pl.ds(pl.multiple_of(q * Q, 16), Q)]

    def over_x(act):
        for j in range(1, 4):
            q = mod(x + j, 4)
            send(act, quarter(xk.at[dp], q), a1.at[x], a1_s.at[j - 1], a1_r.at[x], at(x=q))

    over_x(True)
    keep = pltpu.make_async_copy(quarter(xk.at[dp], x), a1.at[x], own_sem.at[2])
    keep.start()
    keep.wait()

    def plane_of(col):
        return 2 * col + yh // 2, yh % 2

    def to_plane(j, act):
        col = mod(x + j, 4)
        zt, yt = plane_of(col)
        here = jnp.logical_and(zt == z, yt == yl)
        src, dst = a1.at[col], quarter(xd.at[c, dp], x)

        @pl.when(here)
        def _():
            if act:
                pltpu.make_async_copy(src, dst, y_r.at[dp]).start()

        @pl.when(jnp.logical_not(here))
        def _():
            send(act, src, dst, d2_s.at[j], y_r.at[dp], at(z=zt, yl=yt))

    for j in range(4):
        if j:
            col = mod(x + j, 4)
            arrived(a1.at[col], a1_r.at[col])
        to_plane(j, True)

    def columns_rows(n, h, p):
        if h < 3:
            return pl.ds(0, R)
        return pl.ds(n * (R // 2), R // 2)

    def squares_rows(n, h, p):
        if h < 3:
            return pl.ds(GH, GH) if p == 0 else pl.ds(0, GH)
        if p == 2:
            return pl.ds(n * GQ, GQ)
        return (None if n == 0 else pl.ds(GH, GH)) if p == 0 else (pl.ds(0, GH) if n == 0 else None)

    def ring_ref(buf, rows, n, h, p, y, shift):
        zz = mod(z - shift - h, 8) if n == 0 else mod(z + shift + h, 8)
        part = rows(n, h, p)
        return None if part is None else buf.at[2 * zz + y, part]

    def ring_send(act, buf, rows, s, r, h, p, y):
        for n, dev in ((0, up), (1, down)):
            ref = ring_ref(buf, rows, n, h, p, y, 0)
            if ref is not None:
                send(act, ref, ref, s.at[n, h, p], r.at[n, h, p], at(z=dev))

    def ring_wait(buf, rows, r, h, p, y):
        for n in range(2):
            ref = ring_ref(buf, rows, n, h, p, y, 1)
            if ref is not None:
                arrived(ref, r.at[n, h, p])

    def columns_pair(act):
        send(act, xk.at[dp], xk.at[dp], tp_s, tp_r, at(yl=1 - yl))

    def columns_send(act, h, p):
        ring_send(act, xk, columns_rows, t_s, t_r, h, p, yl if p == 0 else 1 - yl)

    def columns_hop(h):
        for p in range(2):
            ring_wait(xk, columns_rows, t_r, h - 1, p, yl if p == 0 else 1 - yl)
            if h < 4:
                columns_send(True, h, p)

    columns_pair(True)
    columns_send(True, 0, 0)
    bit[...] = basis_in[...].T
    weights.wait()
    arrived(xk.at[partner], tp_r)
    columns_send(True, 0, 1)

    root = 2 * (z % 2) + yl
    role = mod(yh - root, 4)
    hops = (role, mod(4 - role, 4))

    def stage(f, i, late):
        g = i - hops[f] * CHAIN - late
        e = 2 * mod(z + offset(g) + 8, 8) + f
        return jnp.logical_and(g >= 0, g < 8), e

    right, left = mod(x + 1, 4), mod(x + 3, 4)
    west, east = at(x=left), at(x=right)

    def spread(f, e, act):
        mine = quarter(xd.at[c, e], x)
        if act:
            arrived(mine, y_r.at[e])

        @pl.when(hops[f] < 3)
        def _():
            step = 1 if f == 0 else 3
            copy = remote(mine, mine, ch_s.at[e], y_r.at[e], at(yh=mod(yh + step, 4)))
            copy.start() if act else copy.wait_send()

        for n, dev in enumerate((east, west)):
            copy = remote(mine, mine, x_s.at[n, e], x_r.at[n, e], dev)
            copy.start() if act else copy.wait_send()

    def across(f, e, act):
        from_left, from_right = quarter(xd.at[c, e], left), quarter(xd.at[c, e], right)
        if act:
            arrived(from_left, x_r.at[0, e])
            arrived(from_right, x_r.at[1, e])
        ref, dev = (from_left, east) if f == 0 else (from_right, west)
        copy = remote(ref, ref, x2_s.at[e], x2_r.at[e], dev)
        copy.start() if act else copy.wait_send()

    def share(f, e, act):
        if act:
            arrived(quarter(xd.at[c, e], mod(x + 2, 4)), x2_r.at[e])
        copy = remote(xd.at[c, e], xd.at[c, e], c_s.at[e], c_r.at[e], at(c=1 - c))
        copy.start() if act else copy.wait_send()

    def pair(zz, act):
        send(act, pb.at[zz], rb.at[zz], pr_s.at[zz], pr_r.at[zz], at(yl=1 - yl))

    def project(g):
        zz = mod(z + offset(g) + 8, 8)
        cols = []
        for f in range(2):
            arrived(xd.at[1 - c, 2 * zz + f], c_r.at[2 * zz + f])
        for f in range(2):
            cols.append(jnp.concatenate([xd[0, 2 * zz + f, 0:G], xd[1, 2 * zz + f, 0:G]], axis=0))
        out = nn(bt[...], jnp.concatenate(cols, axis=1))
        first, second = out[:, 0:B], out[:, B : 2 * B]
        even = yl == 0
        pf[zz] = jnp.where(even, first, second)
        pb[zz] = jnp.where(even, second, first).astype(BF16)
        pair(zz, True)

    def reduce_send(act, s, j):
        for n, (buf, sign, dev) in enumerate(((rsu, -s, up), (rsd, s, down))):
            zz = mod(z + 4 + sign, 8)
            if s == 0:
                part = j + 2 * n
            else:
                part = (j + 2) % 4 if n == 0 else j
            rows = slice(part * GQ, part * GQ + GQ)
            if act:
                if j == 0 and (s > 0 or n == 0):
                    arrived(rb.at[zz], pr_r.at[zz])
                value = pf[zz, rows] + rb[zz, rows].astype(F32)
                if s > 1 or (s == 1 and part // 2 == n):
                    arrived(buf.at[s - 1, rows], rs_r.at[n, s - 1, part])
                    value = value + buf[s - 1, rows]
                pf[zz, rows] = value
            send(act, pf.at[zz, rows], buf.at[s, rows], rs_s.at[n, s, part], rs_r.at[n, s, part], at(z=dev))

    def reduce_end():
        arrived(rb.at[z], pr_r.at[z])
        for part in (0, 2, 1, 3):
            rows = slice(part * GQ, part * GQ + GQ)
            value = pf[z, rows] + rb[z, rows].astype(F32)
            for n, buf in enumerate((rsu, rsd)):
                arrived(buf.at[3, rows], rs_r.at[n, 3, part])
                value = value + buf[3, rows]
            sq[dp, rows] = (value * value).astype(BF16)

    def project_in(act):
        if act:
            mine = bit[pl.ds(pl.multiple_of(c * A, A), A)]
            other = bit[pl.ds(pl.multiple_of((1 - c) * A, A), A)]
            for e in range(0, NB, 4):
                cols = jnp.concatenate([xk[e + n, G:R] for n in range(4)], axis=1)
                for weights, ref in ((mine, pio), (other, pis)):
                    out = nn(weights, cols)
                    for n in range(4):
                        ref[e + n] = out[:, n * B : (n + 1) * B]
        send(act, pis, pir, in_s.at[0], in_r.at[0], at(c=1 - c))

    def in_over_x(act):
        if act:
            arrived(pir, in_r.at[0])
            pio[...] = pio[...] + pir[...]
        for j in range(1, 4):
            q = mod(x + j, 4)
            send(act, pio.at[pl.ds(4 * q, 4)], px.at[x], in_s.at[j], in_r.at[1 + x], at(x=q))

    def in_over_y(act):
        mine = pl.ds(4 * x, 4)
        if act:
            acc = pio[mine]
            for j in range(1, 4):
                q = mod(x + j, 4)
                arrived(px.at[q], in_r.at[1 + q])
                acc = acc + px[q]
            pio[mine] = acc
        for j in range(1, 4):
            w = mod(yh + j, 4)
            send(act, pio.at[4 * x + w], py.at[yh], in_s.at[3 + j], in_r.at[5 + yh], at(yh=w))

    def in_square(act):
        if act:
            acc = pio[k]
            for j in range(1, 4):
                w = mod(yh + j, 4)
                arrived(py.at[w], in_r.at[5 + w])
                acc = acc + py[w]
            si[c, k] = (acc * acc).astype(BF16)
        for j in range(1, 4):
            w = mod(yh + j, 4)
            send(act, si.at[c, k], si.at[c, k], in_s.at[6 + j], in_r.at[9 + yh], at(yh=w))

    def in_gather_x(act):
        if act:
            for j in range(1, 4):
                w = mod(yh + j, 4)
                arrived(si.at[c, 4 * x + w], in_r.at[9 + w])
        mine = si.at[c, pl.ds(4 * x, 4)]
        for j in range(1, 4):
            q = mod(x + j, 4)
            send(act, mine, mine, in_s.at[9 + j], in_r.at[13 + x], at(x=q))

    def in_share(act):
        if act:
            for j in range(1, 4):
                q = mod(x + j, 4)
                arrived(si.at[c, pl.ds(4 * q, 4)], in_r.at[13 + q])
        send(act, si.at[c], si.at[c], in_s.at[13], in_r.at[17], at(c=1 - c))

    def squares_send(act, h, p):
        ring_send(act, sq, squares_rows, g_s, g_r, h, p, yl if p < 2 else 1 - yl)

    def lower(act, zz):
        ref = sq.at[2 * zz + yl, GH:G]
        send(act, ref, ref, gb_s.at[zz], gb_r.at[zz], at(yl=1 - yl))

    def upper(act):
        ref = sq.at[dp, 0:GH]
        send(act, ref, ref, gp_s, gp_r, at(yl=1 - yl))

    def squares_hop(h):
        for p in range(3):
            ring_wait(sq, squares_rows, g_r, h - 1, p, yl if p < 2 else 1 - yl)
            if h < 4:
                squares_send(True, h, p)
            if p == 0:
                for zz in (mod(z - h, 8), mod(z + h, 8))[: 2 if h < 4 else 1]:
                    lower(True, zz)

    scale = 1.0 / (NB * B)

    def covariances(first):
        for e in (first, first + 4):
            blocks = range(e, e + 4)
            rows = jnp.concatenate([xk[n, 0:G] for n in blocks], axis=1)
            cols = jnp.concatenate(
                [jnp.concatenate([xd[0, n, 0:G], xd[1, n, 0:G]], axis=0) for n in blocks], axis=1
            )
            part = nt(rows, cols) * scale
            grad_cov[...] = part if e == 0 else grad_cov[...] + part
            rows = jnp.concatenate([xk[n, G:R] for n in blocks], axis=1)
            cols = jnp.concatenate(
                [jnp.concatenate([xd[0, n, G:R], xd[1, n, G:R]], axis=0) for n in blocks], axis=1
            )
            part = nt(rows, cols) * scale
            act_cov[...] = part if e == 0 else act_cov[...] + part

    def correct(distances):
        places = [mod(z + n, 8) for n in distances]
        for zz in places:
            arrived(sq.at[2 * zz + 1 - yl, GH:G], gb_r.at[zz])
        blocks = [2 * zz + y for zz in places for y in range(2)]
        rows = jnp.concatenate([sq[e] for e in blocks], axis=1)
        cols = jnp.concatenate([jnp.concatenate([si[0, e], si[1, e]], axis=0) for e in blocks], axis=1)
        part = nt(rows, cols) * scale
        corr[...] = part if 0 in distances else corr[...] + part

    def store(act):
        copy = pltpu.make_async_copy(grad_cov, grad_out, own_sem.at[3])
        copy.start() if act else copy.wait()

    work = {}
    for n, when in enumerate(GATHER_AT):
        work.setdefault(when, []).append(functools.partial(columns_hop, n + 1))
    for n in range(4):
        for j in range(2 if n == 0 else 4):
            when = REDUCE_AT + 2 * n + (0 if n == 0 else j // 2)
            work.setdefault(when, []).append(functools.partial(reduce_send, True, n, j))
    for when, fn in zip(INPUT_AT, (project_in, in_over_x)):
        work.setdefault(when, []).append(functools.partial(fn, True))

    def step(i, carry):
        for f in range(2):
            for late, fn in ((0, spread), (K1, across), (K2, share)):
                valid, e = stage(f, i, late)

                @pl.when(valid)
                def _():
                    fn(f, e, True)

        g = i - PROJECT

        @pl.when(jnp.logical_and(g >= 0, g < 8))
        def _():
            project(g)

        for when in sorted(work):
            if when < STEPS:

                @pl.when(i == when)
                def _():
                    for fn in work[when]:
                        fn()

        return carry

    lax.fori_loop(0, STEPS, step, 0)
    for when in sorted(work):
        if when >= STEPS:
            for fn in work[when]:
                fn()

    covariances(0)
    in_over_y(True)

    reduce_end()
    upper(True)
    squares_send(True, 0, 0)
    squares_send(True, 0, 1)
    lower(True, z)
    arrived(sq.at[partner, 0:GH], gp_r)
    squares_send(True, 0, 2)
    in_square(True)
    squares_hop(1)
    in_gather_x(True)
    covariances(8)
    store(True)
    squares_hop(2)
    in_share(True)
    squares_hop(3)
    arrived(si.at[1 - c], in_r.at[17])
    correct((0, 1, 7, 2, 6))
    squares_hop(4)
    correct((3, 5, 4))

    store(False)
    over_x(False)
    for j in range(4):
        to_plane(j, False)
    columns_pair(False)
    upper(False)
    for h in range(4):
        for j in range(2 if h == 0 else 4):
            reduce_send(False, h, j)
        for p in range(2):
            columns_send(False, h, p)
        for p in range(3):
            squares_send(False, h, p)
    for fn in (project_in, in_over_x, in_over_y, in_square, in_gather_x, in_share):
        fn(False)

    def finish(g, carry):
        for f in range(2):
            e = 2 * g + f
            spread(f, e, False)
            across(f, e, False)
            share(f, e, False)
        pair(g, False)
        lower(False, g)
        return carry

    lax.fori_loop(0, 8, finish, 0)


def settle(*refs):
    ins, outs, held, sems = refs[0:3], refs[3:6], refs[6:9], refs[9]
    steps = []
    for n, parts in ((1, 4), (2, 2), (0, 1)):
        rows = ins[n].shape[0] // parts
        for j in range(parts):
            at, m = pl.ds(j * rows, rows), len(steps)
            steps.append(
                (
                    pltpu.make_async_copy(ins[n].at[at], held[n].at[at], sems.at[0, m]),
                    pltpu.make_async_copy(held[n].at[at], outs[n].at[at], sems.at[1, m]),
                )
            )
    for read, _ in steps:
        read.start()
    for read, write in steps:
        read.wait()
        write.start()
    for _, write in steps:
        write.wait()


def body(acts, grads, basis_in, basis_out):
    vmem = pl.BlockSpec(memory_space=pltpu.VMEM)
    hbm = pl.BlockSpec(memory_space=pltpu.HBM)
    dma = pltpu.SemaphoreType.DMA
    shapes = (
        jax.ShapeDtypeStruct((A, 2 * A), F32),
        jax.ShapeDtypeStruct((G, 2 * G), F32),
        jax.ShapeDtypeStruct((G, 2 * A), F32),
    )
    results = pl.pallas_call(
        kernel,
        out_shape=shapes,
        in_specs=[vmem, hbm, vmem, hbm],
        out_specs=(vmem, hbm, vmem),
        scratch_shapes=[
            pltpu.VMEM((NB, R, B), BF16),
            pltpu.VMEM((4, Q, B), BF16),
            pltpu.VMEM((2, NB, R, B), BF16),
            pltpu.VMEM((G, 2 * G), BF16),
            pltpu.VMEM((2 * A, A), BF16),
            pltpu.VMEM((G, 2 * G), F32),
            pltpu.VMEM((8, G, B), F32),
            pltpu.VMEM((8, G, B), BF16),
            pltpu.VMEM((8, G, B), BF16),
            pltpu.VMEM((4, G, B), F32),
            pltpu.VMEM((4, G, B), F32),
            pltpu.VMEM((NB, G, B), BF16),
            pltpu.VMEM((NB, A, B), F32),
            pltpu.VMEM((NB, A, B), F32),
            pltpu.VMEM((NB, A, B), F32),
            pltpu.VMEM((4, 4, A, B), F32),
            pltpu.VMEM((4, A, B), F32),
            pltpu.VMEM((2, NB, A, B), BF16),
            dma((3,)), dma((4,)), dma((4,)), dma((4,)), dma((NB,)), dma((NB,)),
            dma((2, NB)), dma((2, NB)), dma((NB,)), dma((NB,)), dma((NB,)), dma((NB,)),
            dma, dma, dma((2, 4, 2)), dma((2, 4, 2)), dma((8,)), dma((8,)),
            dma((2, 4, 4)), dma((2, 4, 4)), dma, dma, dma((2, 4, 3)), dma((2, 4, 3)), dma((8,)), dma((8,)),
            dma((14,)), dma((18,)),
        ],
        compiler_params=pltpu.CompilerParams(
            collective_id=0, has_side_effects=True, vmem_limit_bytes=62 << 20
        ),
        name="ekfac",
    )(acts, grads.T, basis_in, basis_out.T)
    return pl.pallas_call(
        settle,
        out_shape=shapes,
        in_specs=[hbm] * 3,
        out_specs=(hbm,) * 3,
        scratch_shapes=[pltpu.VMEM(shape.shape, F32) for shape in shapes] + [dma((2, 8))],
        compiler_params=pltpu.CompilerParams(vmem_limit_bytes=62 << 20),
        name="settle",
    )(*results)


def solution(mesh):
    in_specs = (P("dp", "tile"), P("dp", "tile"), P("tile", "dp"), P("dp", "tile"))
    out_specs = (P("tile", "dp"), P("tile", "dp"), P("tile", "dp"))
    return jax.shard_map(body, mesh=mesh, in_specs=in_specs, out_specs=out_specs, check_vma=False)
```

```python
import functools

import jax
import jax.numpy as jnp
from jax import lax
from jax.experimental import pallas as pl
from jax.experimental.pallas import tpu as pltpu
from jax.sharding import PartitionSpec as P

MESH = pl.DeviceIdType.MESH
F32 = jnp.float32
BF16 = jnp.bfloat16

G = 448
A = 128
R = G + A
Q = G // 4
U = A // 4
B = 128
NB = 16
GH = G // 2
GQ = G // 4

CHAIN = 2
K1, K2, K3 = 2, 4, 5
PROJECT = 3 * CHAIN + K3
STEPS = 8 + PROJECT
GATHER_AT = (3, 6, 9, 12)
REDUCE_AT = PROJECT + 1
ACTS_AT = 12
INPUT_AT = (13, 15)


def mod(a, n):
    return (a + n) % n


def nt(a, b):
    return lax.dot_general(a, b, (((1,), (1,)), ((), ())), preferred_element_type=F32)


def nn(a, b):
    return lax.dot_general(a, b, (((1,), (0,)), ((), ())), preferred_element_type=F32)


def arrived(ref, sem):
    pltpu.make_async_copy(ref, ref, sem).wait()


def offset(g):
    half = (g + 1) // 2
    return 4 + half * (1 - 2 * (g % 2))


def kernel(
    acts, grads_t, basis_in, basis_out_t, act_cov, grad_out, corr,
    xk, a1, aa, xd, bt, bit, grad_cov, pf, pb, rb, rsu, rsd, sq, pio, pis, pir, px, py, si,
    a1_s, a1_r, aa_s, aa_r, own_sem, d2_s, da_s, y_r, ya_r, yb_s, yb_r, xa_s, xa_r, xb_s, xb_r, ca_s, ca_r, ch_s, x_s, x_r, x2_s, x2_r, c_s, c_r,
    tp_s, tp_r, t_s, t_r, pr_s, pr_r, rs_s, rs_r, gp_s, gp_r, g_s, g_r, gb_s, gb_r,
    in_s, in_r,
):
    dp, tile = lax.axis_index("dp"), lax.axis_index("tile")
    z, yl = dp // 2, dp % 2
    k, c = tile // 2, tile % 2
    x, yh = k // 4, k % 4
    up, down = mod(z + 1, 8), mod(z + 7, 8)
    partner = 2 * z + 1 - yl

    def at(z=z, yl=yl, x=x, yh=yh, c=c):
        return (2 * z + yl, (4 * x + yh) * 2 + c)

    def remote(src, dst, ss, rs, dev):
        return pltpu.make_async_remote_copy(
            src_ref=src, dst_ref=dst, send_sem=ss, recv_sem=rs, device_id=dev, device_id_type=MESH
        )

    def send(act, src, dst, ss, rs, dev):
        copy = remote(src, dst, ss, rs, dev)
        copy.start() if act else copy.wait_send()

    barrier = pltpu.get_barrier_semaphore()

    def greet(j, carry):
        pl.semaphore_signal(barrier, inc=1, device_id=(mod(dp + j, 16), tile), device_id_type=MESH)
        return carry

    lax.fori_loop(1, 16, greet, 0)
    for j in range(1, 4):
        pl.semaphore_signal(barrier, inc=1, device_id=at(x=mod(x + j, 4)), device_id_type=MESH)
        pl.semaphore_signal(barrier, inc=1, device_id=at(yh=mod(yh + j, 4)), device_id_type=MESH)
    pl.semaphore_signal(barrier, inc=1, device_id=at(c=1 - c), device_id_type=MESH)

    own_grads = pltpu.make_async_copy(grads_t, xk.at[dp, pl.ds(0, G)], own_sem.at[0])
    own_grads.start()
    weights = pltpu.make_async_copy(basis_out_t, bt, own_sem.at[1])
    weights.start()
    xk[dp, G:R] = acts[...].T
    own_grads.wait()
    pl.semaphore_wait(barrier, 22)

    def quarter(ref, q):
        return ref.at[pl.ds(pl.multiple_of(q * Q, 16), Q)]

    def acts_quarter(ref, q):
        return ref.at[pl.ds(pl.multiple_of(G + q * U, 16), U)]

    def over_x(act):
        for j in range(1, 4):
            q = mod(x + j, 4)
            send(act, quarter(xk.at[dp], q), a1.at[x], a1_s.at[j - 1], a1_r.at[x], at(x=q))

    over_x(True)
    keep = pltpu.make_async_copy(quarter(xk.at[dp], x), a1.at[x], own_sem.at[2])
    keep.start()
    keep.wait()

    def acts_over_x(act):
        for j in range(1, 4):
            q = mod(x + j, 4)
            send(act, acts_quarter(xk.at[dp], q), aa.at[x], aa_s.at[j - 1], aa_r.at[x], at(x=q))
        if act:
            copy = pltpu.make_async_copy(acts_quarter(xk.at[dp], x), aa.at[x], own_sem.at[4])
            copy.start()
            copy.wait()

    def plane_of(col):
        return 2 * col + yh // 2, yh % 2

    def to_plane(j, act, whose=0):
        col = mod(x + j, 4)
        zt, yt = plane_of(col)
        here = jnp.logical_and(zt == z, yt == yl)
        place = xd.at[c, yl, z]
        if whose == 0:
            src, dst, ss, rs = a1.at[col], quarter(place, x), d2_s.at[j], y_r.at[dp]
        else:
            src, dst, ss, rs = aa.at[col], acts_quarter(place, x), da_s.at[j], ya_r.at[dp]

        @pl.when(here)
        def _():
            if act:
                pltpu.make_async_copy(src, dst, rs).start()

        @pl.when(jnp.logical_not(here))
        def _():
            send(act, src, dst, ss, rs, at(z=zt, yl=yt))

    for j in range(4):
        if j:
            col = mod(x + j, 4)
            arrived(a1.at[col], a1_r.at[col])
        to_plane(j, True)

    def acts_to_planes():
        for j in range(4):
            if j:
                col = mod(x + j, 4)
                arrived(aa.at[col], aa_r.at[col])
            to_plane(j, True, 1)


    def columns_rows(n, h, p):
        if h < 3:
            return pl.ds(0, R)
        return pl.ds(n * (R // 2), R // 2)

    def squares_rows(n, h, p):
        if h < 3:
            return pl.ds(GH, GH) if p == 0 else pl.ds(0, GH)
        if p == 2:
            return pl.ds(n * GQ, GQ)
        return (None if n == 0 else pl.ds(GH, GH)) if p == 0 else (pl.ds(0, GH) if n == 0 else None)

    def ring_ref(buf, rows, n, h, p, y, shift):
        zz = mod(z - shift - h, 8) if n == 0 else mod(z + shift + h, 8)
        part = rows(n, h, p)
        return None if part is None else buf.at[2 * zz + y, part]

    def ring_send(act, buf, rows, s, r, h, p, y):
        for n, dev in ((0, up), (1, down)):
            ref = ring_ref(buf, rows, n, h, p, y, 0)
            if ref is not None:
                send(act, ref, ref, s.at[n, h, p], r.at[n, h, p], at(z=dev))

    def ring_wait(buf, rows, r, h, p, y):
        for n in range(2):
            ref = ring_ref(buf, rows, n, h, p, y, 1)
            if ref is not None:
                arrived(ref, r.at[n, h, p])

    def columns_pair(act):
        send(act, xk.at[dp], xk.at[dp], tp_s, tp_r, at(yl=1 - yl))

    def columns_send(act, h, p):
        ring_send(act, xk, columns_rows, t_s, t_r, h, p, yl if p == 0 else 1 - yl)

    def columns_hop(h):
        for p in range(2):
            ring_wait(xk, columns_rows, t_r, h - 1, p, yl if p == 0 else 1 - yl)
            if h < 4:
                columns_send(True, h, p)

    columns_pair(True)
    columns_send(True, 0, 0)
    bit[...] = basis_in[...].T
    weights.wait()
    arrived(xk.at[partner], tp_r)
    columns_send(True, 0, 1)

    root = 2 * (z % 2) + yl
    role = mod(yh - root, 4)
    hops = (role, mod(4 - role, 4))

    def stage(f, i, late):
        g = i - hops[f] * CHAIN - late
        e = 2 * mod(z + offset(g) + 8, 8) + f
        return jnp.logical_and(g >= 0, g < 8), e

    right, left = mod(x + 1, 4), mod(x + 3, 4)
    west, east = at(x=left), at(x=right)

    def spread(f, e, act):
        mine = quarter(xd.at[c, f, e // 2], x)
        if act:
            arrived(mine, y_r.at[e])

        @pl.when(hops[f] < 3)
        def _():
            step = 1 if f == 0 else 3
            copy = remote(mine, mine, ch_s.at[e], y_r.at[e], at(yh=mod(yh + step, 4)))
            copy.start() if act else copy.wait_send()

        for n, dev in enumerate((east, west)):
            copy = remote(mine, mine, x_s.at[n, e], x_r.at[n, e], dev)
            copy.start() if act else copy.wait_send()

    def across(f, e, act):
        from_left, from_right = quarter(xd.at[c, f, e // 2], left), quarter(xd.at[c, f, e // 2], right)
        if act:
            arrived(from_left, x_r.at[0, e])
            arrived(from_right, x_r.at[1, e])
        ref, dev = (from_left, east) if f == 0 else (from_right, west)
        copy = remote(ref, ref, x2_s.at[e], x2_r.at[e], dev)
        copy.start() if act else copy.wait_send()

    def share(f, e, act):
        if act:
            arrived(quarter(xd.at[c, f, e // 2], mod(x + 2, 4)), x2_r.at[e])
        ref = xd.at[c, f, e // 2, pl.ds(0, G)]
        send(act, ref, ref, c_s.at[e], c_r.at[e], at(c=1 - c))

    def pair(zz, act):
        send(act, pb.at[zz], rb.at[zz], pr_s.at[zz], pr_r.at[zz], at(yl=1 - yl))

    def acts_ref(f, q):
        return xd.at[c, f, pl.ds(0, 8), pl.ds(pl.multiple_of(G + q * U, 16), U)]

    def acts_spread(f, act):
        ref = acts_ref(f, x)
        if act:

            @pl.when(role == 0)
            def _():
                for zz in range(8):
                    arrived(xd.at[c, f, zz, pl.ds(G, U)], ya_r.at[2 * zz + f])

            @pl.when(role != 0)
            def _():
                arrived(ref, yb_r.at[f])

        @pl.when(hops[f] < 3)
        def _():
            send(act, ref, ref, yb_s.at[f], yb_r.at[f], at(yh=mod(yh + (1 if f == 0 else 3), 4)))

        for n, dev in enumerate((east, west)):
            send(act, ref, ref, xa_s.at[n, f], xa_r.at[n, f], dev)

    def acts_across(act):
        for f in range(2):
            if act:
                arrived(acts_ref(f, left), xa_r.at[0, f])
                arrived(acts_ref(f, right), xa_r.at[1, f])
            ref, dev = (acts_ref(f, left), east) if f == 0 else (acts_ref(f, right), west)
            send(act, ref, ref, xb_s.at[f], xb_r.at[f], dev)

    def acts_share(act):
        for f in range(2):
            if act:
                arrived(acts_ref(f, mod(x + 2, 4)), xb_r.at[f])
            ref = xd.at[c, f, pl.ds(0, 8), pl.ds(G, A)]
            send(act, ref, ref, ca_s.at[f], ca_r.at[f], at(c=1 - c))

    def project(g):
        zz = mod(z + offset(g) + 8, 8)
        cols = []
        for f in range(2):
            arrived(xd.at[1 - c, f, zz, pl.ds(0, G)], c_r.at[2 * zz + f])
        for f in range(2):
            cols.append(jnp.concatenate([xd[0, f, zz, 0:G], xd[1, f, zz, 0:G]], axis=0))
        out = nn(bt[...], jnp.concatenate(cols, axis=1))
        first, second = out[:, 0:B], out[:, B : 2 * B]
        even = yl == 0
        pf[zz] = jnp.where(even, first, second)
        pb[zz] = jnp.where(even, second, first).astype(BF16)
        pair(zz, True)

    def reduce_send(act, s, j):
        for n, (buf, sign, dev) in enumerate(((rsu, -s, up), (rsd, s, down))):
            zz = mod(z + 4 + sign, 8)
            if s == 0:
                part = j + 2 * n
            else:
                part = (j + 2) % 4 if n == 0 else j
            rows = slice(part * GQ, part * GQ + GQ)
            if act:
                if j == 0 and (s > 0 or n == 0):
                    arrived(rb.at[zz], pr_r.at[zz])
                value = pf[zz, rows] + rb[zz, rows].astype(F32)
                if s > 1 or (s == 1 and part // 2 == n):
                    arrived(buf.at[s - 1, rows], rs_r.at[n, s - 1, part])
                    value = value + buf[s - 1, rows]
                pf[zz, rows] = value
            send(act, pf.at[zz, rows], buf.at[s, rows], rs_s.at[n, s, part], rs_r.at[n, s, part], at(z=dev))

    def reduce_end():
        arrived(rb.at[z], pr_r.at[z])
        for part in (0, 2, 1, 3):
            rows = slice(part * GQ, part * GQ + GQ)
            value = pf[z, rows] + rb[z, rows].astype(F32)
            for n, buf in enumerate((rsu, rsd)):
                arrived(buf.at[3, rows], rs_r.at[n, 3, part])
                value = value + buf[3, rows]
            sq[dp, rows] = (value * value).astype(BF16)

    def project_in(act):
        if act:
            mine = bit[pl.ds(pl.multiple_of(c * A, A), A)]
            other = bit[pl.ds(pl.multiple_of((1 - c) * A, A), A)]
            for e in range(0, NB, 4):
                cols = jnp.concatenate([xk[e + n, G:R] for n in range(4)], axis=1)
                for weights, ref in ((mine, pio), (other, pis)):
                    out = nn(weights, cols)
                    for n in range(4):
                        ref[e + n] = out[:, n * B : (n + 1) * B]
        send(act, pis, pir, in_s.at[0], in_r.at[0], at(c=1 - c))

    def in_over_x(act):
        if act:
            arrived(pir, in_r.at[0])
            pio[...] = pio[...] + pir[...]
        for j in range(1, 4):
            q = mod(x + j, 4)
            send(act, pio.at[pl.ds(4 * q, 4)], px.at[x], in_s.at[j], in_r.at[1 + x], at(x=q))

    def in_over_y(act):
        mine = pl.ds(4 * x, 4)
        if act:
            acc = pio[mine]
            for j in range(1, 4):
                q = mod(x + j, 4)
                arrived(px.at[q], in_r.at[1 + q])
                acc = acc + px[q]
            pio[mine] = acc
        for j in range(1, 4):
            w = mod(yh + j, 4)
            send(act, pio.at[4 * x + w], py.at[yh], in_s.at[3 + j], in_r.at[5 + yh], at(yh=w))

    def in_square(act):
        if act:
            acc = pio[k]
            for j in range(1, 4):
                w = mod(yh + j, 4)
                arrived(py.at[w], in_r.at[5 + w])
                acc = acc + py[w]
            si[c, k] = (acc * acc).astype(BF16)
        for j in range(1, 4):
            w = mod(yh + j, 4)
            send(act, si.at[c, k], si.at[c, k], in_s.at[6 + j], in_r.at[9 + yh], at(yh=w))

    def in_gather_x(act):
        if act:
            for j in range(1, 4):
                w = mod(yh + j, 4)
                arrived(si.at[c, 4 * x + w], in_r.at[9 + w])
        mine = si.at[c, pl.ds(4 * x, 4)]
        for j in range(1, 4):
            q = mod(x + j, 4)
            send(act, mine, mine, in_s.at[9 + j], in_r.at[13 + x], at(x=q))

    def in_share(act):
        if act:
            for j in range(1, 4):
                q = mod(x + j, 4)
                arrived(si.at[c, pl.ds(4 * q, 4)], in_r.at[13 + q])
        send(act, si.at[c], si.at[c], in_s.at[13], in_r.at[17], at(c=1 - c))

    def squares_send(act, h, p):
        ring_send(act, sq, squares_rows, g_s, g_r, h, p, yl if p < 2 else 1 - yl)

    def lower(act, zz):
        ref = sq.at[2 * zz + yl, GH:G]
        send(act, ref, ref, gb_s.at[zz], gb_r.at[zz], at(yl=1 - yl))

    def upper(act):
        ref = sq.at[dp, 0:GH]
        send(act, ref, ref, gp_s, gp_r, at(yl=1 - yl))

    def squares_hop(h):
        for p in range(3):
            ring_wait(sq, squares_rows, g_r, h - 1, p, yl if p < 2 else 1 - yl)
            if h < 4:
                squares_send(True, h, p)
            if p == 0:
                for zz in (mod(z - h, 8), mod(z + h, 8))[: 2 if h < 4 else 1]:
                    lower(True, zz)

    scale = 1.0 / (NB * B)

    def covariance(out, low, high, blocks):
        rows = jnp.concatenate([xk[e, low:high] for e in blocks], axis=1)
        cols = jnp.concatenate(
            [
                jnp.concatenate([xd[n, e % 2, e // 2, low:high] for n in range(2)], axis=0)
                for e in blocks
            ],
            axis=1,
        )
        part = nt(rows, cols) * scale
        out[...] = part if 0 in blocks else out[...] + part

    def covariances(first):
        for e in (first, first + 4):
            covariance(grad_cov, 0, G, range(e, e + 4))

    def acts_covariance():
        for f in range(2):
            arrived(xd.at[1 - c, f, pl.ds(0, 8), pl.ds(G, A)], ca_r.at[f])
        for e in (0, 8):
            covariance(act_cov, G, R, range(e, e + 8))

    def correct(distances):
        places = [mod(z + n, 8) for n in distances]
        for zz in places:
            arrived(sq.at[2 * zz + 1 - yl, GH:G], gb_r.at[zz])
        blocks = [2 * zz + y for zz in places for y in range(2)]
        rows = jnp.concatenate([sq[e] for e in blocks], axis=1)
        cols = jnp.concatenate([jnp.concatenate([si[0, e], si[1, e]], axis=0) for e in blocks], axis=1)
        part = nt(rows, cols) * scale
        corr[...] = part if 0 in distances else corr[...] + part

    def store(act):
        copy = pltpu.make_async_copy(grad_cov, grad_out, own_sem.at[3])
        copy.start() if act else copy.wait()

    work = {ACTS_AT - 7: [functools.partial(acts_over_x, True)], ACTS_AT - 5: [acts_to_planes]}
    for n, when in enumerate(GATHER_AT):
        work.setdefault(when, []).append(functools.partial(columns_hop, n + 1))
    for n in range(4):
        for j in range(2 if n == 0 else 4):
            when = REDUCE_AT + 2 * n + (0 if n == 0 else j // 2)
            work.setdefault(when, []).append(functools.partial(reduce_send, True, n, j))
    for when, fn in zip(INPUT_AT, (project_in, in_over_x)):
        work.setdefault(when, []).append(functools.partial(fn, True))

    def step(i, carry):
        for f in range(2):
            for late, fn in ((K2, share), (K1, across), (0, spread)):
                valid, e = stage(f, i, late)

                @pl.when(valid)
                def _():
                    fn(f, e, True)

            @pl.when(i == ACTS_AT + 2 * hops[f])
            def _():
                acts_spread(f, True)

        g = i - PROJECT

        @pl.when(jnp.logical_and(g >= 0, g < 8))
        def _():
            project(g)

        for when in sorted(work):
            if when < STEPS:

                @pl.when(i == when)
                def _():
                    for fn in work[when]:
                        fn()

        return carry

    lax.fori_loop(0, STEPS, step, 0)
    for when in sorted(work):
        if when >= STEPS:
            for fn in work[when]:
                fn()

    covariances(0)
    in_over_y(True)

    reduce_end()
    upper(True)
    squares_send(True, 0, 0)
    squares_send(True, 0, 1)
    lower(True, z)
    arrived(sq.at[partner, 0:GH], gp_r)
    squares_send(True, 0, 2)
    in_square(True)
    squares_hop(1)
    in_gather_x(True)
    covariances(8)
    store(True)
    acts_across(True)
    squares_hop(2)
    in_share(True)
    squares_hop(3)
    acts_share(True)
    arrived(si.at[1 - c], in_r.at[17])
    correct((0, 1, 7, 2, 6))
    acts_covariance()
    squares_hop(4)
    correct((3, 5, 4))

    store(False)
    over_x(False)
    acts_over_x(False)
    for j in range(4):
        to_plane(j, False)
        to_plane(j, False, 1)
    columns_pair(False)
    upper(False)
    for f in range(2):
        acts_spread(f, False)
    acts_across(False)
    acts_share(False)
    for h in range(4):
        for j in range(2 if h == 0 else 4):
            reduce_send(False, h, j)
        for p in range(2):
            columns_send(False, h, p)
        for p in range(3):
            squares_send(False, h, p)
    for fn in (project_in, in_over_x, in_over_y, in_square, in_gather_x, in_share):
        fn(False)

    def finish(g, carry):
        for f in range(2):
            e = 2 * g + f
            spread(f, e, False)
            across(f, e, False)
            share(f, e, False)
        pair(g, False)
        lower(False, g)
        return carry

    lax.fori_loop(0, 8, finish, 0)


def settle(*refs):
    ins, outs, held, sems = refs[0:3], refs[3:6], refs[6:9], refs[9]
    steps = []
    for n, parts in ((1, 4), (2, 2), (0, 1)):
        rows = ins[n].shape[0] // parts
        for j in range(parts):
            at, m = pl.ds(j * rows, rows), len(steps)
            steps.append(
                (
                    pltpu.make_async_copy(ins[n].at[at], held[n].at[at], sems.at[0, m]),
                    pltpu.make_async_copy(held[n].at[at], outs[n].at[at], sems.at[1, m]),
                )
            )
    for read, _ in steps:
        read.start()
    for read, write in steps:
        read.wait()
        write.start()
    for _, write in steps:
        write.wait()


def body(acts, grads, basis_in, basis_out):
    vmem = pl.BlockSpec(memory_space=pltpu.VMEM)
    hbm = pl.BlockSpec(memory_space=pltpu.HBM)
    dma = pltpu.SemaphoreType.DMA
    shapes = (
        jax.ShapeDtypeStruct((A, 2 * A), F32),
        jax.ShapeDtypeStruct((G, 2 * G), F32),
        jax.ShapeDtypeStruct((G, 2 * A), F32),
    )
    results = pl.pallas_call(
        kernel,
        out_shape=shapes,
        in_specs=[vmem, hbm, vmem, hbm],
        out_specs=(vmem, hbm, vmem),
        scratch_shapes=[
            pltpu.VMEM((NB, R, B), BF16),
            pltpu.VMEM((4, Q, B), BF16),
            pltpu.VMEM((4, U, B), BF16),
            pltpu.VMEM((2, 2, 8, R, B), BF16),
            pltpu.VMEM((G, 2 * G), BF16),
            pltpu.VMEM((2 * A, A), BF16),
            pltpu.VMEM((G, 2 * G), F32),
            pltpu.VMEM((8, G, B), F32),
            pltpu.VMEM((8, G, B), BF16),
            pltpu.VMEM((8, G, B), BF16),
            pltpu.VMEM((4, G, B), F32),
            pltpu.VMEM((4, G, B), F32),
            pltpu.VMEM((NB, G, B), BF16),
            pltpu.VMEM((NB, A, B), F32),
            pltpu.VMEM((NB, A, B), F32),
            pltpu.VMEM((NB, A, B), F32),
            pltpu.VMEM((4, 4, A, B), F32),
            pltpu.VMEM((4, A, B), F32),
            pltpu.VMEM((2, NB, A, B), BF16),
            dma((3,)), dma((4,)), dma((3,)), dma((4,)), dma((5,)), dma((4,)), dma((4,)), dma((NB,)), dma((NB,)),
            dma((2,)), dma((2,)), dma((2, 2)), dma((2, 2)), dma((2,)), dma((2,)), dma((2,)), dma((2,)), dma((NB,)),
            dma((2, NB)), dma((2, NB)), dma((NB,)), dma((NB,)), dma((NB,)), dma((NB,)),
            dma, dma, dma((2, 4, 2)), dma((2, 4, 2)), dma((8,)), dma((8,)),
            dma((2, 4, 4)), dma((2, 4, 4)), dma, dma, dma((2, 4, 3)), dma((2, 4, 3)), dma((8,)), dma((8,)),
            dma((14,)), dma((18,)),
        ],
        compiler_params=pltpu.CompilerParams(
            collective_id=0, has_side_effects=True, vmem_limit_bytes=62 << 20
        ),
        name="ekfac",
    )(acts, grads.T, basis_in, basis_out.T)
    return pl.pallas_call(
        settle,
        out_shape=shapes,
        in_specs=[hbm] * 3,
        out_specs=(hbm,) * 3,
        scratch_shapes=[pltpu.VMEM(shape.shape, F32) for shape in shapes] + [dma((2, 8))],
        compiler_params=pltpu.CompilerParams(vmem_limit_bytes=62 << 20),
        name="settle",
    )(*results)


def solution(mesh):
    in_specs = (P("dp", "tile"), P("dp", "tile"), P("tile", "dp"), P("dp", "tile"))
    out_specs = (P("tile", "dp"), P("tile", "dp"), P("tile", "dp"))
    return jax.shard_map(body, mesh=mesh, in_specs=in_specs, out_specs=out_specs, check_vma=False)
```

```python
import functools

import jax
import jax.numpy as jnp
from jax import lax
from jax.experimental import pallas as pl
from jax.experimental.pallas import tpu as pltpu
from jax.sharding import PartitionSpec as P

MESH = pl.DeviceIdType.MESH
F32 = jnp.float32
BF16 = jnp.bfloat16

G = 448
A = 128
R = G + A
Q = G // 4
U = A // 4
B = 128
NB = 16
GH = G // 2
GQ = G // 4
GS = 336

CHAIN = 2
K1, K2, K3 = 2, 4, 5
PROJECT = 3 * CHAIN + K3
STEPS = 8 + PROJECT
GATHER_AT = (3, 6, 9, 12)
REDUCE_AT = PROJECT + 1
ACTS_AT = 12
INPUT_AT = (12, 15)


def mod(a, n):
    return (a + n) % n


def nt(a, b):
    return lax.dot_general(a, b, (((1,), (1,)), ((), ())), preferred_element_type=F32)


def nn(a, b):
    return lax.dot_general(a, b, (((1,), (0,)), ((), ())), preferred_element_type=F32)


def arrived(ref, sem):
    pltpu.make_async_copy(ref, ref, sem).wait()


def offset(g):
    half = (g + 1) // 2
    return 4 + half * (1 - 2 * (g % 2))


def kernel(
    acts, grads_t, basis_in, basis_out_t, act_cov, grad_out, corr,
    xk, a1, aa, xd, bt, bit, grad_cov, pf, pb, rb, rsu, rsd, sq, pio, pis, pir, px, py, si,
    a1_s, a1_r, aa_s, aa_r, own_sem, d2_s, da_s, y_r, ya_r, yb_s, yb_r, xa_s, xa_r, xb_s, xb_r, ca_s, ca_r, ch_s, x_s, x_r, x2_s, x2_r, c_s, c_r,
    tp_s, tp_r, t_s, t_r, pr_s, pr_r, rs_s, rs_r, gp_s, gp_r, g_s, g_r, gb_s, gb_r,
    in_s, in_r,
):
    dp, tile = lax.axis_index("dp"), lax.axis_index("tile")
    z, yl = dp // 2, dp % 2
    k, c = tile // 2, tile % 2
    x, yh = k // 4, k % 4
    up, down = mod(z + 1, 8), mod(z + 7, 8)
    partner = 2 * z + 1 - yl

    def at(z=z, yl=yl, x=x, yh=yh, c=c):
        return (2 * z + yl, (4 * x + yh) * 2 + c)

    def remote(src, dst, ss, rs, dev):
        return pltpu.make_async_remote_copy(
            src_ref=src, dst_ref=dst, send_sem=ss, recv_sem=rs, device_id=dev, device_id_type=MESH
        )

    def send(act, src, dst, ss, rs, dev):
        copy = remote(src, dst, ss, rs, dev)
        copy.start() if act else copy.wait_send()

    barrier = pltpu.get_barrier_semaphore()

    def greet(j, carry):
        pl.semaphore_signal(barrier, inc=1, device_id=(mod(dp + j, 16), tile), device_id_type=MESH)
        return carry

    lax.fori_loop(1, 16, greet, 0)
    for j in range(1, 4):
        pl.semaphore_signal(barrier, inc=1, device_id=at(x=mod(x + j, 4)), device_id_type=MESH)
        pl.semaphore_signal(barrier, inc=1, device_id=at(yh=mod(yh + j, 4)), device_id_type=MESH)
    pl.semaphore_signal(barrier, inc=1, device_id=at(c=1 - c), device_id_type=MESH)

    own_grads = pltpu.make_async_copy(grads_t, xk.at[dp, pl.ds(0, G)], own_sem.at[0])
    own_grads.start()
    weights = pltpu.make_async_copy(basis_out_t, bt, own_sem.at[1])
    weights.start()
    xk[dp, G:R] = acts[...].T
    own_grads.wait()
    pl.semaphore_wait(barrier, 22)

    def quarter(ref, q):
        return ref.at[pl.ds(pl.multiple_of(q * Q, 16), Q)]

    def acts_quarter(ref, q):
        return ref.at[pl.ds(pl.multiple_of(G + q * U, 16), U)]

    def over_x(act):
        for j in range(1, 4):
            q = mod(x + j, 4)
            send(act, quarter(xk.at[dp], q), a1.at[x], a1_s.at[j - 1], a1_r.at[x], at(x=q))

    over_x(True)
    keep = pltpu.make_async_copy(quarter(xk.at[dp], x), a1.at[x], own_sem.at[2])
    keep.start()
    keep.wait()

    def acts_over_x(act):
        for j in range(1, 4):
            q = mod(x + j, 4)
            send(act, acts_quarter(xk.at[dp], q), aa.at[x], aa_s.at[j - 1], aa_r.at[x], at(x=q))
        if act:
            copy = pltpu.make_async_copy(acts_quarter(xk.at[dp], x), aa.at[x], own_sem.at[4])
            copy.start()
            copy.wait()

    def plane_of(col):
        return 2 * col + yh // 2, yh % 2

    def to_plane(j, act, whose=0):
        col = mod(x + j, 4)
        zt, yt = plane_of(col)
        here = jnp.logical_and(zt == z, yt == yl)
        place = xd.at[c, yl, z]
        if whose == 0:
            src, dst, ss, rs = a1.at[col], quarter(place, x), d2_s.at[j], y_r.at[dp]
        else:
            src, dst, ss, rs = aa.at[col], acts_quarter(place, x), da_s.at[j], ya_r.at[dp]

        @pl.when(here)
        def _():
            if act:
                pltpu.make_async_copy(src, dst, rs).start()

        @pl.when(jnp.logical_not(here))
        def _():
            send(act, src, dst, ss, rs, at(z=zt, yl=yt))

    for j in range(4):
        if j:
            col = mod(x + j, 4)
            arrived(a1.at[col], a1_r.at[col])
        to_plane(j, True)

    def acts_to_planes():
        for j in range(4):
            if j:
                col = mod(x + j, 4)
                arrived(aa.at[col], aa_r.at[col])
            to_plane(j, True, 1)


    def columns_rows(n, h, p):
        if h < 3:
            return pl.ds(0, R)
        return pl.ds(n * (R // 2), R // 2)

    def squares_rows(n, h, p):
        if h < 3:
            low, high = (GS, G) if p == 0 else (0, GS)
        elif p == 2:
            low, high = ((0, GS // 32 * 16), (GS // 32 * 16, GS))[n]
        else:
            low, high = (((G, G), (GS, G)), ((0, GH), (GH, GS)))[p][n]
        return None if low == high else pl.ds(low, high - low)

    def ring_ref(buf, rows, n, h, p, y, shift):
        zz = mod(z - shift - h, 8) if n == 0 else mod(z + shift + h, 8)
        part = rows(n, h, p)
        return None if part is None else buf.at[2 * zz + y, part]

    def ring_send(act, buf, rows, s, r, h, p, y):
        for n, dev in ((0, up), (1, down)):
            ref = ring_ref(buf, rows, n, h, p, y, 0)
            if ref is not None:
                send(act, ref, ref, s.at[n, h, p], r.at[n, h, p], at(z=dev))

    def ring_wait(buf, rows, r, h, p, y):
        for n in range(2):
            ref = ring_ref(buf, rows, n, h, p, y, 1)
            if ref is not None:
                arrived(ref, r.at[n, h, p])

    def columns_pair(act):
        send(act, xk.at[dp], xk.at[dp], tp_s, tp_r, at(yl=1 - yl))

    def columns_send(act, h, p):
        ring_send(act, xk, columns_rows, t_s, t_r, h, p, yl if p == 0 else 1 - yl)

    def columns_hop(h):
        for p in range(2):
            ring_wait(xk, columns_rows, t_r, h - 1, p, yl if p == 0 else 1 - yl)
            if h < 4:
                columns_send(True, h, p)

    columns_pair(True)
    columns_send(True, 0, 0)
    bit[...] = basis_in[...].T
    weights.wait()
    arrived(xk.at[partner], tp_r)
    columns_send(True, 0, 1)

    root = 2 * (z % 2) + yl
    role = mod(yh - root, 4)
    hops = (role, mod(4 - role, 4))

    def stage(f, i, late):
        g = i - hops[f] * CHAIN - late
        e = 2 * mod(z + offset(g) + 8, 8) + f
        return jnp.logical_and(g >= 0, g < 8), e

    right, left = mod(x + 1, 4), mod(x + 3, 4)
    west, east = at(x=left), at(x=right)

    def spread(f, e, act):
        mine = quarter(xd.at[c, f, e // 2], x)
        if act:
            arrived(mine, y_r.at[e])

        @pl.when(hops[f] < 3)
        def _():
            step = 1 if f == 0 else 3
            copy = remote(mine, mine, ch_s.at[e], y_r.at[e], at(yh=mod(yh + step, 4)))
            copy.start() if act else copy.wait_send()

        for n, dev in enumerate((east, west)):
            copy = remote(mine, mine, x_s.at[n, e], x_r.at[n, e], dev)
            copy.start() if act else copy.wait_send()

    def across(f, e, act):
        from_left, from_right = quarter(xd.at[c, f, e // 2], left), quarter(xd.at[c, f, e // 2], right)
        if act:
            arrived(from_left, x_r.at[0, e])
            arrived(from_right, x_r.at[1, e])
        ref, dev = (from_left, east) if f == 0 else (from_right, west)
        copy = remote(ref, ref, x2_s.at[e], x2_r.at[e], dev)
        copy.start() if act else copy.wait_send()

    def share(f, e, act):
        if act:
            arrived(quarter(xd.at[c, f, e // 2], mod(x + 2, 4)), x2_r.at[e])
        ref = xd.at[c, f, e // 2, pl.ds(0, G)]
        send(act, ref, ref, c_s.at[e], c_r.at[e], at(c=1 - c))

    def pair(zz, act):
        send(act, pb.at[zz], rb.at[zz], pr_s.at[zz], pr_r.at[zz], at(yl=1 - yl))

    def acts_ref(f, q):
        return xd.at[c, f, pl.ds(0, 8), pl.ds(pl.multiple_of(G + q * U, 16), U)]

    def acts_spread(f, act):
        ref = acts_ref(f, x)
        if act:

            @pl.when(role == 0)
            def _():
                for zz in range(8):
                    arrived(xd.at[c, f, zz, pl.ds(G, U)], ya_r.at[2 * zz + f])

            @pl.when(role != 0)
            def _():
                arrived(ref, yb_r.at[f])

        @pl.when(hops[f] < 3)
        def _():
            send(act, ref, ref, yb_s.at[f], yb_r.at[f], at(yh=mod(yh + (1 if f == 0 else 3), 4)))

        for n, dev in enumerate((east, west)):
            send(act, ref, ref, xa_s.at[n, f], xa_r.at[n, f], dev)

    def acts_across(act):
        for f in range(2):
            if act:
                arrived(acts_ref(f, left), xa_r.at[0, f])
                arrived(acts_ref(f, right), xa_r.at[1, f])
            ref, dev = (acts_ref(f, left), east) if f == 0 else (acts_ref(f, right), west)
            send(act, ref, ref, xb_s.at[f], xb_r.at[f], dev)

    def acts_share(act):
        for f in range(2):
            if act:
                arrived(acts_ref(f, mod(x + 2, 4)), xb_r.at[f])
            ref = xd.at[c, f, pl.ds(0, 8), pl.ds(G, A)]
            send(act, ref, ref, ca_s.at[f], ca_r.at[f], at(c=1 - c))

    def project(g):
        zz = mod(z + offset(g) + 8, 8)
        cols = []
        for f in range(2):
            arrived(xd.at[1 - c, f, zz, pl.ds(0, G)], c_r.at[2 * zz + f])
        for f in range(2):
            cols.append(jnp.concatenate([xd[0, f, zz, 0:G], xd[1, f, zz, 0:G]], axis=0))
        out = nn(bt[...], jnp.concatenate(cols, axis=1))
        first, second = out[:, 0:B], out[:, B : 2 * B]
        even = yl == 0
        pf[zz] = jnp.where(even, first, second)
        pb[zz] = jnp.where(even, second, first).astype(BF16)
        pair(zz, True)

    def reduce_send(act, s, j):
        for n, (buf, sign, dev) in enumerate(((rsu, -s, up), (rsd, s, down))):
            zz = mod(z + 4 + sign, 8)
            if s == 0:
                part = j + 2 * n
            else:
                part = (j + 2) % 4 if n == 0 else j
            rows = slice(part * GQ, part * GQ + GQ)
            if act:
                if j == 0 and (s > 0 or n == 0):
                    arrived(rb.at[zz], pr_r.at[zz])
                value = pf[zz, rows] + rb[zz, rows].astype(F32)
                if s > 1 or (s == 1 and part // 2 == n):
                    arrived(buf.at[s - 1, rows], rs_r.at[n, s - 1, part])
                    value = value + buf[s - 1, rows]
                pf[zz, rows] = value
            send(act, pf.at[zz, rows], buf.at[s, rows], rs_s.at[n, s, part], rs_r.at[n, s, part], at(z=dev))

    def reduce_end():
        arrived(rb.at[z], pr_r.at[z])
        for part in (0, 2, 1, 3):
            rows = slice(part * GQ, part * GQ + GQ)
            value = pf[z, rows] + rb[z, rows].astype(F32)
            for n, buf in enumerate((rsu, rsd)):
                arrived(buf.at[3, rows], rs_r.at[n, 3, part])
                value = value + buf[3, rows]
            sq[dp, rows] = (value * value).astype(BF16)

    def project_in(act):
        if act:
            mine = bit[pl.ds(pl.multiple_of(c * A, A), A)]
            other = bit[pl.ds(pl.multiple_of((1 - c) * A, A), A)]
            for e in range(0, NB, 4):
                cols = jnp.concatenate([xk[e + n, G:R] for n in range(4)], axis=1)
                for weights, ref in ((mine, pio), (other, pis)):
                    out = nn(weights, cols)
                    for n in range(4):
                        ref[e + n] = out[:, n * B : (n + 1) * B]
        send(act, pis, pir, in_s.at[0], in_r.at[0], at(c=1 - c))

    def in_over_x(act):
        if act:
            arrived(pir, in_r.at[0])
            pio[...] = pio[...] + pir[...]
        for j in range(1, 4):
            q = mod(x + j, 4)
            send(act, pio.at[pl.ds(4 * q, 4)], px.at[x], in_s.at[j], in_r.at[1 + x], at(x=q))

    def in_over_y(act):
        mine = pl.ds(4 * x, 4)
        if act:
            acc = pio[mine]
            for j in range(1, 4):
                q = mod(x + j, 4)
                arrived(px.at[q], in_r.at[1 + q])
                acc = acc + px[q]
            pio[mine] = acc
        for j in range(1, 4):
            w = mod(yh + j, 4)
            send(act, pio.at[4 * x + w], py.at[yh], in_s.at[3 + j], in_r.at[5 + yh], at(yh=w))

    def in_square(act):
        if act:
            acc = pio[k]
            for j in range(1, 4):
                w = mod(yh + j, 4)
                arrived(py.at[w], in_r.at[5 + w])
                acc = acc + py[w]
            si[c, k] = (acc * acc).astype(BF16)
        for j in range(1, 4):
            w = mod(yh + j, 4)
            send(act, si.at[c, k], si.at[c, k], in_s.at[6 + j], in_r.at[9 + yh], at(yh=w))

    def in_gather_x(act):
        if act:
            for j in range(1, 4):
                w = mod(yh + j, 4)
                arrived(si.at[c, 4 * x + w], in_r.at[9 + w])
        mine = si.at[c, pl.ds(4 * x, 4)]
        for j in range(1, 4):
            q = mod(x + j, 4)
            send(act, mine, mine, in_s.at[9 + j], in_r.at[13 + x], at(x=q))

    def in_share(act):
        if act:
            for j in range(1, 4):
                q = mod(x + j, 4)
                arrived(si.at[c, pl.ds(4 * q, 4)], in_r.at[13 + q])
        send(act, si.at[c], si.at[c], in_s.at[13], in_r.at[17], at(c=1 - c))

    def squares_send(act, h, p):
        ring_send(act, sq, squares_rows, g_s, g_r, h, p, yl if p < 2 else 1 - yl)

    def lower(act, zz):
        ref = sq.at[2 * zz + yl, GS:G]
        send(act, ref, ref, gb_s.at[zz], gb_r.at[zz], at(yl=1 - yl))

    def upper(act):
        ref = sq.at[dp, 0:GS]
        send(act, ref, ref, gp_s, gp_r, at(yl=1 - yl))

    def squares_hop(h):
        for p in range(3):
            ring_wait(sq, squares_rows, g_r, h - 1, p, yl if p < 2 else 1 - yl)
            if h < 4:
                squares_send(True, h, p)
            if p == 0:
                for zz in (mod(z - h, 8), mod(z + h, 8))[: 2 if h < 4 else 1]:
                    lower(True, zz)

    scale = 1.0 / (NB * B)

    def covariance(out, low, high, blocks):
        rows = jnp.concatenate([xk[e, low:high] for e in blocks], axis=1)
        cols = jnp.concatenate(
            [
                jnp.concatenate([xd[n, e % 2, e // 2, low:high] for n in range(2)], axis=0)
                for e in blocks
            ],
            axis=1,
        )
        part = nt(rows, cols) * scale
        out[...] = part if 0 in blocks else out[...] + part

    def covariances(first):
        for e in (first, first + 4):
            covariance(grad_cov, 0, G, range(e, e + 4))

    def acts_covariance():
        for f in range(2):
            arrived(xd.at[1 - c, f, pl.ds(0, 8), pl.ds(G, A)], ca_r.at[f])
        for e in (0, 8):
            covariance(act_cov, G, R, range(e, e + 8))

    def correct(distances):
        places = [mod(z + n, 8) for n in distances]
        for zz in places:
            arrived(sq.at[2 * zz + 1 - yl, GS:G], gb_r.at[zz])
        blocks = [2 * zz + y for zz in places for y in range(2)]
        rows = jnp.concatenate([sq[e] for e in blocks], axis=1)
        cols = jnp.concatenate([jnp.concatenate([si[0, e], si[1, e]], axis=0) for e in blocks], axis=1)
        part = nt(rows, cols) * scale
        corr[...] = part if 0 in distances else corr[...] + part

    def store(act):
        copy = pltpu.make_async_copy(grad_cov, grad_out, own_sem.at[3])
        copy.start() if act else copy.wait()

    work = {ACTS_AT - 7: [functools.partial(acts_over_x, True)], ACTS_AT - 5: [acts_to_planes]}
    for n, when in enumerate(GATHER_AT):
        work.setdefault(when, []).append(functools.partial(columns_hop, n + 1))
    for n in range(4):
        for j in range(2 if n == 0 else 4):
            when = REDUCE_AT + 2 * n + (0 if n == 0 else j // 2)
            work.setdefault(when, []).append(functools.partial(reduce_send, True, n, j))
    for when, fn in zip(INPUT_AT, (project_in, in_over_x)):
        work.setdefault(when, []).append(functools.partial(fn, True))

    def step(i, carry):
        for f in range(2):
            for late, fn in ((K2, share), (K1, across), (0, spread)):
                valid, e = stage(f, i, late)

                @pl.when(valid)
                def _():
                    fn(f, e, True)

            @pl.when(i == ACTS_AT + 2 * hops[f])
            def _():
                acts_spread(f, True)

        g = i - PROJECT

        @pl.when(jnp.logical_and(g >= 0, g < 8))
        def _():
            project(g)

        for when in sorted(work):
            if when < STEPS:

                @pl.when(i == when)
                def _():
                    for fn in work[when]:
                        fn()

        return carry

    lax.fori_loop(0, STEPS, step, 0)
    for when in sorted(work):
        if when >= STEPS:
            for fn in work[when]:
                fn()

    covariances(0)
    in_over_y(True)

    reduce_end()
    upper(True)
    squares_send(True, 0, 0)
    squares_send(True, 0, 1)
    lower(True, z)
    arrived(sq.at[partner, 0:GS], gp_r)
    squares_send(True, 0, 2)
    in_square(True)
    squares_hop(1)
    in_gather_x(True)
    covariances(8)
    store(True)
    acts_across(True)
    squares_hop(2)
    in_share(True)
    squares_hop(3)
    acts_share(True)
    arrived(si.at[1 - c], in_r.at[17])
    correct((0, 1, 7, 2, 6))
    acts_covariance()
    squares_hop(4)
    correct((3, 5, 4))

    store(False)
    over_x(False)
    acts_over_x(False)
    for j in range(4):
        to_plane(j, False)
        to_plane(j, False, 1)
    columns_pair(False)
    upper(False)
    for f in range(2):
        acts_spread(f, False)
    acts_across(False)
    acts_share(False)
    for h in range(4):
        for j in range(2 if h == 0 else 4):
            reduce_send(False, h, j)
        for p in range(2):
            columns_send(False, h, p)
        for p in range(3):
            squares_send(False, h, p)
    for fn in (project_in, in_over_x, in_over_y, in_square, in_gather_x, in_share):
        fn(False)

    def finish(g, carry):
        for f in range(2):
            e = 2 * g + f
            spread(f, e, False)
            across(f, e, False)
            share(f, e, False)
        pair(g, False)
        lower(False, g)
        return carry

    lax.fori_loop(0, 8, finish, 0)


def settle(*refs):
    ins, outs, held, sems = refs[0:3], refs[3:6], refs[6:9], refs[9]
    steps = []
    for n, parts in ((1, 4), (2, 2), (0, 1)):
        rows = ins[n].shape[0] // parts
        for j in range(parts):
            at, m = pl.ds(j * rows, rows), len(steps)
            steps.append(
                (
                    pltpu.make_async_copy(ins[n].at[at], held[n].at[at], sems.at[0, m]),
                    pltpu.make_async_copy(held[n].at[at], outs[n].at[at], sems.at[1, m]),
                )
            )
    for read, _ in steps:
        read.start()
    for read, write in steps:
        read.wait()
        write.start()
    for _, write in steps:
        write.wait()


def body(acts, grads, basis_in, basis_out):
    vmem = pl.BlockSpec(memory_space=pltpu.VMEM)
    hbm = pl.BlockSpec(memory_space=pltpu.HBM)
    dma = pltpu.SemaphoreType.DMA
    shapes = (
        jax.ShapeDtypeStruct((A, 2 * A), F32),
        jax.ShapeDtypeStruct((G, 2 * G), F32),
        jax.ShapeDtypeStruct((G, 2 * A), F32),
    )
    results = pl.pallas_call(
        kernel,
        out_shape=shapes,
        in_specs=[vmem, hbm, vmem, hbm],
        out_specs=(vmem, hbm, vmem),
        scratch_shapes=[
            pltpu.VMEM((NB, R, B), BF16),
            pltpu.VMEM((4, Q, B), BF16),
            pltpu.VMEM((4, U, B), BF16),
            pltpu.VMEM((2, 2, 8, R, B), BF16),
            pltpu.VMEM((G, 2 * G), BF16),
            pltpu.VMEM((2 * A, A), BF16),
            pltpu.VMEM((G, 2 * G), F32),
            pltpu.VMEM((8, G, B), F32),
            pltpu.VMEM((8, G, B), BF16),
            pltpu.VMEM((8, G, B), BF16),
            pltpu.VMEM((4, G, B), F32),
            pltpu.VMEM((4, G, B), F32),
            pltpu.VMEM((NB, G, B), BF16),
            pltpu.VMEM((NB, A, B), F32),
            pltpu.VMEM((NB, A, B), F32),
            pltpu.VMEM((NB, A, B), F32),
            pltpu.VMEM((4, 4, A, B), F32),
            pltpu.VMEM((4, A, B), F32),
            pltpu.VMEM((2, NB, A, B), BF16),
            dma((3,)), dma((4,)), dma((3,)), dma((4,)), dma((5,)), dma((4,)), dma((4,)), dma((NB,)), dma((NB,)),
            dma((2,)), dma((2,)), dma((2, 2)), dma((2, 2)), dma((2,)), dma((2,)), dma((2,)), dma((2,)), dma((NB,)),
            dma((2, NB)), dma((2, NB)), dma((NB,)), dma((NB,)), dma((NB,)), dma((NB,)),
            dma, dma, dma((2, 4, 2)), dma((2, 4, 2)), dma((8,)), dma((8,)),
            dma((2, 4, 4)), dma((2, 4, 4)), dma, dma, dma((2, 4, 3)), dma((2, 4, 3)), dma((8,)), dma((8,)),
            dma((14,)), dma((18,)),
        ],
        compiler_params=pltpu.CompilerParams(
            collective_id=0, has_side_effects=True, vmem_limit_bytes=62 << 20
        ),
        name="ekfac",
    )(acts, grads.T, basis_in, basis_out.T)
    return pl.pallas_call(
        settle,
        out_shape=shapes,
        in_specs=[hbm] * 3,
        out_specs=(hbm,) * 3,
        scratch_shapes=[pltpu.VMEM(shape.shape, F32) for shape in shapes] + [dma((2, 8))],
        compiler_params=pltpu.CompilerParams(vmem_limit_bytes=62 << 20),
        name="settle",
    )(*results)


def solution(mesh):
    in_specs = (P("dp", "tile"), P("dp", "tile"), P("tile", "dp"), P("dp", "tile"))
    out_specs = (P("tile", "dp"), P("tile", "dp"), P("tile", "dp"))
    return jax.shard_map(body, mesh=mesh, in_specs=in_specs, out_specs=out_specs, check_vma=False)
```
